32 devices in a mesh: dp: 8 (over z, x), tensor: 4 (over y, core).
Axes of the slice: x: 2, y: 2, z: 4, core: 2. Of those that a mesh axis runs over, the one named last changes fastest.
Arguments:
- tokens: bfloat16 [8192, 1024], P('dp'), may hold values from -6 to 6
- segments: int32 [8192], P('dp'), may hold values from -1 to 26, as said below
- cotangent: bfloat16 [8192, 1024], P('dp'), may hold values from -6 to 6
- param_heads: float32 [3, 1024, 1024], P(None, 'dp', 'tensor'), may hold values from -0.1875 to 0.1875
- param_biases: float32 [2, 128, 8], P(None, 'tensor', 'dp'), may hold values from -1.5 to 1.5
- param_mixer: float32 [1024, 1024], P('tensor', 'dp'), may hold values from -1.5 to 1.5
- param_expand: float32 [1024, 4096], P('dp', 'tensor'), may hold values from -0.1875 to 0.1875
- param_offset: float32 [512, 8], P('tensor', 'dp'), may hold values from -2.5 to 2.5
- param_shrink: float32 [4096, 1024], P('tensor', 'dp'), may hold values from -0.09375 to 0.09375
- param_vector: float32 [8, 1024], P(None, 'dp'), may hold values from -0.8 to 1.6
- moment_heads: float32 [3, 1024, 1024], P(None, 'dp', 'tensor'), may hold values from -100 to 100
- moment_biases: float32 [2, 128, 8], P(None, 'tensor', 'dp'), may hold values from -100 to 100
- moment_mixer: float32 [1024, 1024], P('tensor', 'dp'), may hold values from -100 to 100
- moment_expand: float32 [1024, 4096], P('dp', 'tensor'), may hold values from -100 to 100
- moment_offset: float32 [512, 8], P('tensor', 'dp'), may hold values from -100 to 100
- moment_shrink: float32 [4096, 1024], P('tensor', 'dp'), may hold values from -100 to 100
- moment_vector: float32 [8, 1024], P(None, 'dp'), may hold values from -100 to 100
- square_heads: float32 [3, 1024, 1024], P(None, 'dp', 'tensor'), may hold values from 100 to 100000
- square_biases: float32 [2, 128, 8], P(None, 'tensor', 'dp'), may hold values from 100 to 100000
- square_mixer: float32 [1024, 1024], P('tensor', 'dp'), may hold values from 100 to 100000
- square_expand: float32 [1024, 4096], P('dp', 'tensor'), may hold values from 100 to 100000
- square_offset: float32 [512, 8], P('tensor', 'dp'), may hold values from 100 to 100000
- square_shrink: float32 [4096, 1024], P('tensor', 'dp'), may hold values from 100 to 100000
- square_vector: float32 [8, 1024], P(None, 'dp'), may hold values from 100 to 100000
Outputs:
- layer_output: bfloat16 [8192, 1024], P('dp')
- input_gradient: bfloat16 [8192, 1024], P('dp')
- direction_heads: float32 [3, 1024, 1024], P(None, 'dp', 'tensor')
- direction_biases: float32 [2, 128, 8], P(None, 'tensor', 'dp')
- direction_mixer: float32 [1024, 1024], P('tensor', 'dp')
- direction_expand: float32 [1024, 4096], P('dp', 'tensor')
- direction_offset: float32 [512, 8], P('tensor', 'dp')
- direction_shrink: float32 [4096, 1024], P('tensor', 'dp')
- direction_vector: float32 [8, 1024], P(None, 'dp')
- momentum_heads: float32 [3, 1024, 1024], P(None, 'dp', 'tensor')
- momentum_biases: float32 [2, 128, 8], P(None, 'tensor', 'dp')
- momentum_mixer: float32 [1024, 1024], P('tensor', 'dp')
- momentum_expand: float32 [1024, 4096], P('dp', 'tensor')
- momentum_offset: float32 [512, 8], P('tensor', 'dp')
- momentum_shrink: float32 [4096, 1024], P('tensor', 'dp')
- momentum_vector: float32 [8, 1024], P(None, 'dp')
The draws below stay inside these ranges and needn't reach their ends.
Inputs may be any that keep to these rules, and one draw needn't show every extreme that they name: `segments`: in each packed row of 1024 tokens the tokens with one nonnegative number form one contiguous item of 197 or 37 tokens; numbers count up from 0 along the row, and the row ends with one or more padding tokens numbered -1.
All inputs are finite; a program needn't handle non-finite values.
Results may differ from the reference program's by a relative error of at most 0.017.
Values may be sent and summed in bfloat16 or wider, within the bound.
A program may use at most 128 MiB of HBM per device.

```python
import math
import jax
import jax.numpy as jnp
from jax import lax

D = 1024
HEADS = 16
FF = 4096
HEAD = 64
ROW = 1024
ITEM_BIG = 197
ITEM_SMALL = 37
TOKENS = 8192
N_DP = 8


def draw_segments(key, part):
    key = jax.random.fold_in(key, 5)
    kind_key, row_key = jax.random.split(key)
    row_total = TOKENS // ROW
    slot_count = ROW // ITEM_SMALL + 1
    kinds = jax.random.randint(kind_key, (row_total, slot_count), 0, 2)
    chosen_row = jax.random.randint(row_key, (), 0, row_total)
    kinds = jnp.where(jnp.arange(row_total)[:, None] == chosen_row, 0, kinds)
    lengths = jnp.where(kinds == 1, ITEM_BIG, ITEM_SMALL).astype(jnp.int32)
    ends = jnp.cumsum(lengths, axis=1)
    fits = ends <= ROW - 1
    positions = jnp.arange(ROW).astype(jnp.int32)
    passed = (fits[:, None, :] & (ends[:, None, :] <= positions[None, :, None])).astype(jnp.int32)
    numbers = jnp.sum(passed, axis=2)
    used = jnp.max(jnp.where(fits, ends, 0), axis=1)
    numbers = jnp.where(positions[None, :] < used[:, None], numbers, -1)
    return numbers.reshape(TOKENS).astype(jnp.int32)


def draw_param_vector(key, part):
    key = jax.random.fold_in(key, 11)
    first_key, second_key = jax.random.split(key)
    scales = jax.random.uniform(first_key, (8, D), jnp.float32, 0.5, 1.5)
    shifts = jnp.clip(0.2 * jax.random.normal(second_key, (8, D), jnp.float32), -0.8, 0.8)
    rows = jnp.arange(8)[:, None]
    is_scale = (rows == 0) | (rows == 3) | (rows == 4) | (rows == 7)
    return jnp.where(is_scale, scales, shifts)


def raised(values, own_key, source, target, parts, factor):
    def block_of(dim):
        return (jnp.arange(values.shape[dim]) // (values.shape[dim] // parts)).reshape((-1,) + (1,) * (values.ndim - 1 - dim))

    one_side = jax.random.permutation(own_key, parts)[block_of(target)]
    far = (block_of(target) + parts // 2) % parts
    return jnp.where((block_of(source) == one_side) | (block_of(source) == far), factor * values, values)


def shard_levels(stream_key, dims, cuts, low, largest):
    loudness = 1.0
    for position, blocks in cuts:
        steps = jax.random.uniform(jax.random.fold_in(jax.random.fold_in(stream_key, 6), position), (blocks,), jnp.float32, low / len(cuts), largest / len(cuts))
        loudness = loudness * jnp.repeat(jnp.exp(steps), dims[position] // blocks).reshape((-1,) + (1,) * (len(dims) - 1 - position))
    return loudness


def noise(key, dims, spread, most, shards=(), kind=jnp.bfloat16):
    level = shard_levels(key, dims, shards, -0.22, 0.18) if shards else 1.0
    entries = jax.random.normal(key, dims, jnp.float32) * spread * level
    return jnp.minimum(jnp.maximum(entries, -most), most).astype(kind)


def bell_draw_with(own_key, shape, spread, limit, cuts, heavy, kind=jnp.bfloat16):
    drawn = spread * jax.random.normal(own_key, shape, jnp.float32)
    if cuts:
        drawn = drawn * shard_levels(own_key, shape, cuts, -0.22, 0.18)
    return jnp.clip(raised(drawn, jax.random.fold_in(own_key, 3), *heavy), -limit, limit).astype(kind)


def setup_inputs(seed: int = 0) -> dict:
    arg_keys = jax.random.split(jax.random.key(seed), 25)
    tokens = noise(arg_keys[0], (TOKENS, D), 1.0, 6.0, ((0, 8),))
    segments = draw_segments(jax.random.fold_in(arg_keys[24], 71), 0)
    cotangent = bell_draw_with(arg_keys[2], (TOKENS, D), 1.0, 6.0, ((0, 8),), (0, 1, 8, 2.0))
    param_heads = noise(arg_keys[3], (3, D, D), D ** -0.5, 0.1875, ((1, 8), (2, 4)), jnp.float32)
    param_biases = noise(arg_keys[4], (2, D // N_DP, N_DP), 0.3, 1.5, ((1, 4), (2, 8)), jnp.float32)
    param_mixer = noise(arg_keys[5], (D, D), (D // 64) ** -0.5, 1.5, ((0, 4), (1, 8)), jnp.float32)
    param_expand = noise(arg_keys[6], (D, FF), D ** -0.5, 0.1875, ((0, 8), (1, 4)), jnp.float32)
    param_offset = noise(arg_keys[7], (FF // N_DP, N_DP), 0.5, 2.5, ((0, 4), (1, 8)), jnp.float32)
    param_shrink = noise(arg_keys[8], (FF, D), FF ** -0.5, 0.09375, ((0, 4), (1, 8)), jnp.float32)
    param_vector = draw_param_vector(jax.random.fold_in(arg_keys[24], 71), 0)
    moment_heads = noise(arg_keys[10], (3, D, D), 20.0, 100.0, ((1, 8), (2, 4)), jnp.float32)
    moment_biases = noise(arg_keys[11], (2, D // N_DP, N_DP), 20.0, 100.0, ((1, 4), (2, 8)), jnp.float32)
    moment_mixer = noise(arg_keys[12], (D, D), 20.0, 100.0, ((0, 4), (1, 8)), jnp.float32)
    moment_expand = noise(arg_keys[13], (D, FF), 20.0, 100.0, ((0, 8), (1, 4)), jnp.float32)
    moment_offset = noise(arg_keys[14], (FF // N_DP, N_DP), 20.0, 100.0, ((0, 4), (1, 8)), jnp.float32)
    moment_shrink = noise(arg_keys[15], (FF, D), 20.0, 100.0, ((0, 4), (1, 8)), jnp.float32)
    moment_vector = noise(arg_keys[16], (8, D), 20.0, 100.0, ((1, 8),), jnp.float32)
    square_heads = jnp.clip(jnp.exp(math.log(100000.0) - 6.9077553 * jax.random.uniform(arg_keys[17], (3, D, D), jnp.float32) ** shard_levels(arg_keys[17], (3, D, D), ((1, 8), (2, 4)), -0.2, 0.2)), 100.0, 100000.0)
    square_biases = jnp.clip(jnp.exp(math.log(100000.0) - 6.9077553 * jax.random.uniform(arg_keys[18], (2, D // N_DP, N_DP), jnp.float32) ** shard_levels(arg_keys[18], (2, D // N_DP, N_DP), ((1, 4), (2, 8)), -0.2, 0.2)), 100.0, 100000.0)
    square_mixer = jnp.clip(jnp.exp(math.log(100000.0) - 6.9077553 * jax.random.uniform(arg_keys[19], (D, D), jnp.float32) ** shard_levels(arg_keys[19], (D, D), ((0, 4), (1, 8)), -0.2, 0.2)), 100.0, 100000.0)
    square_expand = jnp.clip(jnp.exp(math.log(100000.0) - 6.9077553 * jax.random.uniform(arg_keys[20], (D, FF), jnp.float32) ** shard_levels(arg_keys[20], (D, FF), ((0, 8), (1, 4)), -0.2, 0.2)), 100.0, 100000.0)
    square_offset = jnp.clip(jnp.exp(math.log(100000.0) - 6.9077553 * jax.random.uniform(arg_keys[21], (FF // N_DP, N_DP), jnp.float32) ** shard_levels(arg_keys[21], (FF // N_DP, N_DP), ((0, 4), (1, 8)), -0.2, 0.2)), 100.0, 100000.0)
    square_shrink = jnp.clip(jnp.exp(math.log(100000.0) - 6.9077553 * jax.random.uniform(arg_keys[22], (FF, D), jnp.float32) ** shard_levels(arg_keys[22], (FF, D), ((0, 4), (1, 8)), -0.2, 0.2)), 100.0, 100000.0)
    square_vector = jnp.clip(jnp.exp(math.log(100000.0) - 6.9077553 * jax.random.uniform(arg_keys[23], (8, D), jnp.float32) ** shard_levels(arg_keys[23], (8, D), ((1, 8),), -0.2, 0.2)), 100.0, 100000.0)
    return {"tokens": tokens, "segments": segments, "cotangent": cotangent, "param_heads": param_heads, "param_biases": param_biases, "param_mixer": param_mixer, "param_expand": param_expand, "param_offset": param_offset, "param_shrink": param_shrink, "param_vector": param_vector, "moment_heads": moment_heads, "moment_biases": moment_biases, "moment_mixer": moment_mixer, "moment_expand": moment_expand, "moment_offset": moment_offset, "moment_shrink": moment_shrink, "moment_vector": moment_vector, "square_heads": square_heads, "square_biases": square_biases, "square_mixer": square_mixer, "square_expand": square_expand, "square_offset": square_offset, "square_shrink": square_shrink, "square_vector": square_vector}


@jax.custom_vjp
def low(v):
    return lax.optimization_barrier(v.astype(jnp.bfloat16)).astype(jnp.float32)

@jax.custom_vjp
def low_back(v):
    return v

def low_keep(v):
    return (low(v), None)

def low_pass(kept, grad):
    return (grad,)

def back_keep(v):
    return (v, None)

def back_low(kept, grad):
    return (low(grad),)
low.defvjp(low_keep, low_pass)
low_back.defvjp(back_keep, back_low)
NORM_EPS = 1e-06
NEGATIVE = -1e+30
BETA_ONE = 0.9
BETA_TWO = 0.999
ADAM_EPS = 1e-08
WEIGHT_DECAY = 0.05
CORRECT_ONE = 0.9999734386011124
CORRECT_TWO = 0.0952078528862904

def layer_norm(stream, gain, shift):
    center = stream - lax.optimization_barrier(jnp.mean(stream, -1, keepdims=True))
    variance = lax.optimization_barrier(jnp.mean(center * center, -1, keepdims=True))
    return center * lax.rsqrt(variance + NORM_EPS) * gain + shift

def attend_row(inputs):
    queries, key_rows, value_rows, seg_row = inputs
    block_size = min(512, ROW)
    scaling = HEAD ** (-0.5)
    positions = jnp.arange(ROW).astype(jnp.int32)
    highest = lax.Precision.HIGHEST

    def score_block(start):
        query_block = lax.dynamic_slice_in_dim(queries, start, block_size, 0)
        seg_block = lax.dynamic_slice_in_dim(seg_row, start, block_size, 0)
        scores = jnp.einsum('qhd,khd->hqk', query_block, key_rows, precision=highest) * scaling
        scores = low_back(scores)
        same_item = (seg_block[:, None] == seg_row[None, :]) & (seg_block[:, None] >= 0)
        own_place = (start + jnp.arange(block_size).astype(jnp.int32))[:, None] == positions[None, :]
        scores = jnp.where((same_item | own_place)[None], scores, NEGATIVE)
        chances = jax.nn.softmax(scores, axis=-1)
        return jnp.einsum('hqk,khd->qhd', low(chances), value_rows, precision=highest)
    starts = (jnp.arange(ROW // block_size) * block_size).astype(jnp.int32)
    blocks = lax.map(jax.checkpoint(score_block), starts)
    return blocks.reshape(ROW, HEADS * HEAD)

def forward(stream, seg_rows, heads, biases, mixer, expand, offset, shrink, vector):
    highest = lax.Precision.HIGHEST
    heads = low(heads)
    biases = low(biases).reshape(2, D)
    mixer = low(mixer)
    expand = low(expand)
    offset = low(offset).reshape(FF)
    shrink = low(shrink)
    vector = low(vector)
    normed_one = low(layer_norm(stream, vector[0], vector[1]))
    queries = low_back(low(jnp.dot(normed_one, heads[0], precision=highest) + biases[0]))
    key_rows = low_back(low(jnp.dot(normed_one, heads[1], precision=highest)))
    value_rows = low_back(low(jnp.dot(normed_one, heads[2], precision=highest) + biases[1]))
    shaped = (seg_rows.shape[0], ROW, HEADS, HEAD)
    mixed_heads = lax.map(jax.checkpoint(attend_row), (queries.reshape(shaped), key_rows.reshape(shaped), value_rows.reshape(shaped), seg_rows))
    mixed_heads = low_back(low(mixed_heads.reshape(-1, D)))
    attn_out = low_back(jnp.dot(mixed_heads, mixer, precision=highest) + vector[2])
    middle = stream + vector[3] * attn_out
    normed_two = low(layer_norm(middle, vector[4], vector[5]))
    pre_act = low_back(jnp.dot(normed_two, expand, precision=highest) + offset)
    activation = low(jax.nn.gelu(pre_act, approximate=False))
    mlp_out = low_back(jnp.dot(activation, shrink, precision=highest) + vector[6])
    return middle + vector[7] * mlp_out

def adamw(master, gradient, moment, square, decay_rate):
    moment = BETA_ONE * moment + (1.0 - BETA_ONE) * gradient
    square = BETA_TWO * square + (1.0 - BETA_TWO) * gradient * gradient
    change = moment / CORRECT_ONE / (jnp.sqrt(square / CORRECT_TWO) + ADAM_EPS)
    return (change + decay_rate * master, moment)

def reference(tokens, segments, cotangent, param_heads, param_biases, param_mixer, param_expand, param_offset, param_shrink, param_vector, moment_heads, moment_biases, moment_mixer, moment_expand, moment_offset, moment_shrink, moment_vector, square_heads, square_biases, square_mixer, square_expand, square_offset, square_shrink, square_vector):
    masters = (param_heads, param_biases, param_mixer, param_expand, param_offset, param_shrink, param_vector)
    moments = (moment_heads, moment_biases, moment_mixer, moment_expand, moment_offset, moment_shrink, moment_vector)
    squares = (square_heads, square_biases, square_mixer, square_expand, square_offset, square_shrink, square_vector)
    row_total = TOKENS // ROW
    per_group = min(max(1, 4096 // ROW), row_total)
    groups = row_total // per_group
    streams = tokens.astype(jnp.float32).reshape(groups, per_group * ROW, D)
    pulls = cotangent.astype(jnp.float32).reshape(groups, per_group * ROW, D)
    seg_groups = segments.reshape(groups, per_group, ROW)

    def group_step(totals, inputs):
        stream, seg_rows, pull_back = inputs

        def local(stream_in, *weights):
            return forward(stream_in, seg_rows, *weights)
        result, backward = jax.vjp(local, stream, *masters)
        gradients = backward(pull_back)
        totals = tuple((total + gradient for total, gradient in zip(totals, gradients[1:])))
        return (totals, (result, gradients[0]))
    starting = tuple((jnp.zeros_like(master) for master in masters))
    sums, (results, stream_grads) = lax.scan(group_step, starting, (streams, seg_groups, pulls))
    layer_output = results.reshape(TOKENS, D).astype(jnp.bfloat16)
    input_gradient = stream_grads.reshape(TOKENS, D).astype(jnp.bfloat16)
    decays = (WEIGHT_DECAY, 0.0, WEIGHT_DECAY, WEIGHT_DECAY, 0.0, WEIGHT_DECAY, 0.0)
    stepped = [adamw(masters[slot], sums[slot], moments[slot], squares[slot], decays[slot]) for slot in range(7)]
    return (layer_output, input_gradient, stepped[0][0], stepped[1][0], stepped[2][0], stepped[3][0], stepped[4][0], stepped[5][0], stepped[6][0], stepped[0][1], stepped[1][1], stepped[2][1], stepped[3][1], stepped[4][1], stepped[5][1], stepped[6][1])
```

```python
import functools

import jax
import jax.numpy as jnp
from jax import lax
from jax.experimental import pallas as pl
from jax.experimental.pallas import tpu as pltpu
from jax.sharding import PartitionSpec as P

MESH = pl.DeviceIdType.MESH
WIDE, NARROW = jnp.float32, jnp.bfloat16

HEAD = 64
BLOCK = 256
WINDOW = 768
SMALL_ROWS = 16
VMEM_LIMIT = 66 * 1024 * 1024
LANES = 128

NORM_EPS = 1e-06
NEGATIVE = -1e30
INV_ROOT_TAU = 0.3989422804014327
BETA_ONE = 0.9
BETA_TWO = 0.999
ADAM_EPS = 1e-08
WEIGHT_DECAY = 0.05
CORRECT_ONE = 0.9999734386011124
CORRECT_TWO = 0.0952078528862904

HA, HB, MIX, EXP, SHR = 0, 1, 2, 3, 4

PLAN = {
    "start": [("begin", HB)],
    "cast": [("own", EXP)],
    "small": [("step", HA, 1)],
    "norm0": [("begin", MIX)],
    "norm1": [("step", HA, 2)],
    "norm2": [("step", HB, 1), ("step", MIX, 1)],
    "norm3": [("step", HA, 3), ("begin", EXP), ("step", HB, 2)],
    "mine": [("own", HB)],
    "first0": [("step", MIX, 2)],
    "one0": [("step", HB, 3)],
    "one1": [("own", MIX), ("step", MIX, 3), ("step", EXP, 1)],
    "one2": [("turn", EXP)],
    "two0": [("begin", SHR)],
    "two1": [("own", SHR), ("step", EXP, 2), ("late", EXP, 1)],
    "two2": [("step", EXP, 3), ("step", SHR, 1)],
    "two3": [("late", EXP, 2), ("turn", SHR)],
    "z2": [("late", EXP, 3), ("step", SHR, 2)],
    "expand1": [("late", SHR, 1), ("step", SHR, 3)],
    "expand2": [("late", SHR, 2)],
    "shrink2": [("late", SHR, 3)],
    "grow0": [("on", SHR, 1)],
    "grow2": [("leave", EXP, 0)],
    "grow3": [("on", SHR, 2)],
    "back0": [("on", SHR, 3), ("leave", EXP, 1), ("leave", EXP, 2)],
    "back1": [("leave", EXP, 3)],
    "back2": [("on", EXP, 1)],
    "back3": [("on", EXP, 2)],
    "heads": [("on", EXP, 3), ("on", MIX, 1), ("on", MIX, 2)],
    "y": [("on", MIX, 3), ("on", HA, 1), ("on", HB, 1), ("on", HA, 2), ("on", HB, 2)],
    "dx": [("on", HA, 3), ("on", HB, 3)],
    "pack": [("end", SHR), ("end", EXP)],
    "last": [("end", MIX), ("end", HA), ("end", HB)],
}


def dot(a, b):
    return jnp.dot(a, b, preferred_element_type=WIDE)


def dot_nt(a, b):
    return lax.dot_general(a, b, (((1,), (1,)), ((), ())), preferred_element_type=WIDE)


def dot_tn(a, b):
    return lax.dot_general(a, b, (((0,), (0,)), ((), ())), preferred_element_type=WIDE)


def loop(count, body):
    lax.fori_loop(0, count, lambda i, _: (body(i), None)[1], None)


def normalize(stream):
    center = stream - jnp.mean(stream, -1, keepdims=True)
    inverse = lax.rsqrt(jnp.mean(center * center, -1, keepdims=True) + NORM_EPS)
    return center * inverse, inverse


def norm_back(grad, gain, unit, inverse):
    scaled = grad * gain
    return inverse * (
        scaled - jnp.mean(scaled, -1, keepdims=True) - unit * jnp.mean(scaled * unit, -1, keepdims=True)
    )


def gelu_parts(u):
    bell = jnp.exp(-0.5 * u * u)
    base = 1.0 + (0.3275911 * 0.7071067811865476) * jnp.abs(u)
    t = pl.reciprocal(base, approx=True)
    t = t * (2.0 - base * t)
    poly = t * (
        0.5 * 0.254829592
        + t * (-0.5 * 0.284496736 + t * (0.5 * 1.421413741 + t * (-0.5 * 1.453152027 + t * (0.5 * 1.061405429))))
    )
    tail = poly * bell
    cdf = jnp.where(u >= 0, 1.0 - tail, tail)
    return u * cdf, cdf + u * bell * INV_ROOT_TAU


def fold(x):
    return jnp.sum(x.reshape(x.shape[0] // 8, 8, x.shape[1]), 0)


def kernel(
    nd,
    nt,
    tokens,
    seg_row,
    cotangent,
    own_qkv,
    own_mix,
    own_exp,
    own_shr,
    own_vec,
    own_bias,
    own_off,
    out_y,
    out_dx,
    out_ha,
    out_hb,
    out_mix,
    out_exp,
    out_shr,
    out_small,
    l_mix,
    l_shr,
    w_ha,
    w_hb,
    w_mix,
    w_exp,
    w_shr,
    z1,
    dm,
    x_own,
    c_own,
    seg_col,
    vec,
    bias,
    n1,
    r1,
    q,
    k,
    v,
    kt,
    vt,
    probs,
    inv,
    ot,
    o,
    acc,
    x1,
    att,
    n2,
    r2,
    z2,
    h,
    slope,
    da,
    ds,
    q_split,
    do_split,
    dqkv,
    dk,
    dv,
    comb,
    sums,
    bias_sums,
    row_own,
    sb,
    rb1,
    s2,
    rb2,
    m_acc,
    m_sb,
    m_rb1,
    m_s2,
    m_rb2,
    g_ha,
    g_hb,
    g_mix,
    g_exp,
    g_shr,
    p_ha,
    p_hb,
    p_mix,
    p_exp,
    p_shr,
    f_ha,
    f_hb,
    f_mix,
    f_exp,
    f_shr,
    small_in,
    vec_parts,
    small_send,
    small_recv,
    local_sem,
    ag_rs,
    ag_rr,
    ag_ls,
    ag_lr,
    ag_brs,
    ag_brr,
    ag_bls,
    ag_blr,
    ag_xs,
    ag_xr,
    rs_zs,
    rs_zr,
    rs_xs,
    rs_xr,
    sm_s,
    sm_r,
    gs_s,
    gs_r,
    vs_s,
    vs_r,
    red_s,
    red_r,
    gat_s,
    gat_r,
):
    T, D = z1.shape
    C = q.shape[1]
    F = h.shape[1]
    no = nd // 2
    cs = D // nd
    heads = C // HEAD
    blocks = D // BLOCK
    pairs = BLOCK // (2 * cs)
    own = T // nt

    me = lax.axis_index("dp")
    t = lax.axis_index("tensor")
    mz = me // 2
    mx = me % 2
    x_peer = me + 1 - 2 * mx
    mate = t + 1 - 2 * (t % 2)
    cross = (t + 2) % nt
    far = mate + 2 - 4 * (mate // 2)

    weights = (w_ha, w_hb, w_mix, w_exp, w_shr)
    grads = (g_ha, g_hb, g_mix, g_exp, g_shr)
    firsts = (p_ha, p_hb, p_mix, p_exp, p_shr)
    seconds = (f_ha, f_hb, f_mix, f_exp, f_shr)
    finals = (out_ha, out_hb, out_mix, out_exp, out_shr)
    half = C // 2
    width = 3 * half

    def rows_of(i):
        return pl.ds(pl.multiple_of(i * own, own), own)

    def chunk(ref, i):
        return ref.at[:, pl.ds(pl.multiple_of(i * cs, cs), cs), :]

    def to_dp(src, dst, send, recv, peer):
        return pltpu.make_async_remote_copy(
            src_ref=src, dst_ref=dst, send_sem=send, recv_sem=recv, device_id={"dp": peer}, device_id_type=MESH
        )

    def to_tensor(src, dst, send, recv, peer):
        return pltpu.make_async_remote_copy(
            src_ref=src, dst_ref=dst, send_sem=send, recv_sem=recv, device_id={"tensor": peer}, device_id_type=MESH
        )

    def load(i, src, dst):
        return pltpu.make_async_copy(src, dst, local_sem.at[i])

    loads = [
        load(0, own_mix, l_mix),
        load(1, own_exp, x1.at[0:cs, :]),
        load(2, own_shr, l_shr),
        load(3, tokens, z1),
        load(4, tokens.at[rows_of(t), :], x_own),
        load(5, cotangent, dm),
        load(6, cotangent.at[rows_of(t), :], c_own),
        *[load(7 + j, own_qkv.at[j], att.at[0:cs, j * C : (j + 1) * C]) for j in range(3)],
    ]
    for copy in loads[7:] + loads[:7]:
        copy.start()

    barrier = pltpu.get_barrier_semaphore()

    def greet_dp(i):
        pl.semaphore_signal(barrier, inc=1, device_id={"dp": (me + 1 + i) % nd}, device_id_type=MESH)

    def greet_tensor(i):
        pl.semaphore_signal(barrier, inc=1, device_id={"tensor": (t + 1 + i) % nt}, device_id_type=MESH)

    loop(nd - 1, greet_dp)
    loop(nt - 1, greet_tensor)

    small_in[me] = jnp.zeros_like(small_in[me])
    small_in[me, 0:8, 0:cs] = own_vec[...].astype(NARROW).astype(WIDE)
    small_in[me, 8:10, 0 : own_bias.shape[1]] = own_bias[...].astype(NARROW).astype(WIDE)
    small_in[me, 10:11, 0 : own_off.shape[1]] = own_off[...].astype(NARROW).astype(WIDE)
    for copy in loads[7:]:
        copy.wait()
    mine = pl.ds(pl.multiple_of(me * cs, cs), cs)
    for p in range(2):
        for j in range(3):
            own_part = att[0:cs, j * C + p * half : j * C + (p + 1) * half]
            weights[p][0, mine, j * half : (j + 1) * half] = own_part.astype(NARROW)
    loads[0].wait()
    w_mix[0, mine, :] = l_mix[...].T.astype(NARROW)

    pl.semaphore_wait(barrier, nd + nt - 2)

    turned = (0, 0, 0, F // 4, F // 4)

    def columns(a, i, late):
        width = weights[a].shape[2]
        split = width - turned[a]
        lanes = pl.ds(split, turned[a]) if late else pl.ds(0, split)
        return weights[a].at[:, pl.ds(pl.multiple_of(i * cs, cs), cs), lanes]

    def ag_own(a):
        slot = chunk(weights[a], me)
        return to_dp(slot, slot, ag_xs.at[a, mz], ag_xr.at[a, mz], x_peer)

    def ag_x(a, source):
        slot = columns(a, source * 2 + mx, False)
        return to_dp(slot, slot, ag_xs.at[a, source], ag_xr.at[a, source], x_peer)

    def ag_right(a, d, late=False):
        source = (mz + no + 1 - d) % no
        slot = columns(a, source * 2 + 1 - mx, True) if late else chunk(weights[a], source * 2 + mx)
        send, recv = (ag_brs, ag_brr) if late else (ag_rs, ag_rr)
        return to_dp(slot, slot, send.at[a, d], recv.at[a, d], ((mz + 1) % no) * 2 + mx)

    def ag_left(a, d, late=False):
        source = (mz + d - 1) % no
        slot = columns(a, source * 2 + 1 - mx, True) if late else chunk(weights[a], source * 2 + mx)
        send, recv = (ag_bls, ag_blr) if late else (ag_ls, ag_lr)
        return to_dp(slot, slot, send.at[a, d], recv.at[a, d], ((mz + no - 1) % no) * 2 + mx)

    def ag_leave(a, late):
        @pl.when(mz + 1 < no)
        def _():
            ag_right(a, 1, late).start()

        @pl.when(mz > 0)
        def _():
            ag_left(a, 1, late).start()

    def ag_begin(a):
        ag_leave(a, False)

    def ag_turn(a):
        ag_own(a).wait_recv()
        ag_leave(a, True)

    def ag_step(a, d, late=False):
        @pl.when(mz >= d)
        def _():
            ag_right(a, d, late).wait_recv()

            @pl.when(mz + 1 < no)
            def _():
                ag_right(a, d + 1, late).start()

            if not late:
                ag_x(a, mz - d).start()

        @pl.when(mz + d < no)
        def _():
            ag_left(a, d, late).wait_recv()

            @pl.when(mz > 0)
            def _():
                ag_left(a, d + 1, late).start()

            if not late:
                ag_x(a, mz + d).start()

    def thirds(j, body):
        low, high = 1 + (j - 1) * (no - 1) // 3, 1 + j * (no - 1) // 3
        lax.fori_loop(low, high, lambda i, _: (body(i), None)[1], None)

    def ag_third(a, j, late=False):
        if turned[a] or not late:
            thirds(j, lambda d: ag_step(a, d, late))

    def ag_finish(a):
        if not turned[a]:
            ag_own(a).wait_recv()
        peers(lambda i: ag_x(a, (mz + i) % no).wait_recv())

    def peers(body):
        loop(no - 1, lambda i: body(i + 1))

    def rs_x(a, zz):
        return to_dp(
            chunk(grads[a], zz * 2 + 1 - mx), firsts[a].at[zz], rs_xs.at[a, zz], rs_xr.at[a, zz], x_peer
        )

    def rs_z(a, kk):
        zz = (mz + kk) % no
        return to_dp(firsts[a].at[zz], seconds[a].at[kk - 1], rs_zs.at[a, kk], rs_zr.at[a, kk], zz * 2 + mx)

    def add_step(width):
        return min(cs, 128 if width <= 256 else 32)

    def rs_forward(a, kk):
        zz = (mz + kk) % no
        rs_x(a, zz).wait_recv()
        here = chunk(grads[a], zz * 2 + mx)
        step = add_step(here.shape[2])

        def add(c):
            r = pl.ds(pl.multiple_of(c * step, step), step)
            total = here[0, r, :].astype(WIDE) + firsts[a][zz, 0, r, :].astype(WIDE)
            firsts[a][zz, 0, r, :] = total.astype(NARROW)

        loop(cs // step, add)
        rs_z(a, kk).start()

    def rs_third(a, j):
        thirds(j, lambda kk: rs_forward(a, kk))

    def rs_finish(a):
        rs_x(a, mz).wait_recv()
        loop(no - 1, lambda i: rs_z(a, i + 1).wait_recv())
        here = chunk(grads[a], me)
        step = add_step(here.shape[2])

        def add(c):
            r = pl.ds(pl.multiple_of(c * step, step), step)
            total = here[0, r, :].astype(WIDE) + firsts[a][mz, 0, r, :].astype(WIDE)
            if no <= 4:
                for kk in range(no - 1):
                    total = total + seconds[a][kk, 0, r, :].astype(WIDE)
            else:
                total = lax.fori_loop(
                    0, no - 1, lambda kk, partial: partial + seconds[a][kk, 0, r, :].astype(WIDE), total
                )
            finals[a][0, r, :] = total

        loop(cs // step, add)

    def grad_block_done(a, b):
        loop(pairs, lambda j: rs_x(a, b * pairs + j).start())

    def grad_order(s):
        return (mz // pairs + 1 + s) % blocks

    steps = {
        "begin": ag_begin,
        "own": lambda a: ag_own(a).start(),
        "step": ag_third,
        "turn": ag_turn,
        "late": lambda a, j: ag_third(a, j, True),
        "leave": lambda a, j: grad_block_done(a, grad_order(j)),
        "on": rs_third,
        "end": rs_finish,
    }

    def due(place):
        for name, *args in PLAN.get(place, ()):
            steps[name](*args)

    def due_at(place, s):
        for j in range(nt):
            if place + str(j) in PLAN:

                @pl.when(s == j)
                def _():
                    due(place + str(j))

    bufs = ((sb, rb1, s2, rb2, acc), (m_sb, m_rb1, m_s2, m_rb2, m_acc))

    part_rows = own // 2

    def red(c, j):
        send, first, pair, second, _ = bufs[c]
        if j >= 2:
            rows = slice((j - 2) * part_rows, (j - 1) * part_rows)
            return to_tensor(pair.at[rows, :], second.at[rows, :], red_s.at[c, j], red_r.at[c, j], cross)
        return to_tensor(send.at[j], first.at[j], red_s.at[c, j], red_r.at[c, j], mate)

    def red_block(s):
        second = (s % 2) * 1
        first_half = far + (cross - far) * second
        last_half = mate + (t - mate) * second
        return first_half + (last_half - first_half) * (s // 2)

    def red_step(c, s):
        send, first, pair, _, total = bufs[c]

        @pl.when(s == 0)
        def _():
            send[0] = total[...].astype(NARROW)
            red(c, 0).start()

        @pl.when(s == 1)
        def _():
            red(c, 0).wait_recv()
            for hh in range(2):
                rows = slice(hh * part_rows, (hh + 1) * part_rows)
                pair[rows, :] = (total[rows, :] + first[0, rows, :].astype(WIDE)).astype(NARROW)
                if c == 0:
                    red(c, 2 + hh).start()

        @pl.when(s == 2)
        def _():
            send[1] = total[...].astype(NARROW)
            red(c, 1).start()

    def red_wait(c, hh):
        if hh == 0:
            red(c, 1).wait_recv()
        red(c, 2 + hh).wait_recv()

    def red_drain(c):
        for j in range(4):
            red(c, j).wait_send()

    def red_rows(c, r):
        _, first, _, second, total = bufs[c]
        return total[r, :] + first[1, r, :].astype(WIDE) + second[r, :].astype(WIDE)

    def gat(g, src, ref, j):
        if j == 0:
            return to_tensor(src, ref.at[rows_of(t), :], gat_s.at[g, 0], gat_r.at[g, 0], mate)
        if j == 1:
            block = ref.at[rows_of(cross), :]
            return to_tensor(block, block, gat_s.at[g, 1], gat_r.at[g, 1], mate)
        rows = slice((j - 2) * part_rows, (j - 1) * part_rows)
        there = pl.ds(pl.multiple_of(t * own + (j - 2) * part_rows, part_rows), part_rows)
        return to_tensor(src.at[rows, :], ref.at[there, :], gat_s.at[g, j], gat_r.at[g, j], cross)

    def in_halves(c, g, src, ref, body):
        steps = own // 64 // 2
        for hh in range(2):
            red_wait(c, hh)
            lax.fori_loop(hh * steps, (hh + 1) * steps, lambda i, _: (body(i), None)[1], None)
            gat(g, src, ref, 2 + hh).start()
        gat(g, src, ref, 0).start()
        ref[rows_of(t), :] = src[...]
        red_drain(c)

    def gat_forward(g, src, ref):
        for hh in range(2):
            gat(g, src, ref, 2 + hh).wait_recv()
        gat(g, src, ref, 1).start()

    def small(kk):
        return to_dp(small_in.at[me], small_in.at[me], sm_s.at[kk], sm_r.at[kk], (me + kk) % nd)

    loop(nd - 1, lambda i: small(i + 1).start())
    ag_begin(HA)
    ag_own(HA).start()
    due("start")
    loads[1].wait()
    w_exp[0, mine, :] = x1[0:cs, :].astype(NARROW)
    loads[2].wait()
    w_shr[0, mine, :] = l_shr[...].T.astype(NARROW)
    due("cast")

    place = lax.broadcasted_iota(jnp.int32, (1, T), 1)
    marks = seg_row[...]
    marks = jnp.where(marks >= 0, marks, -1 - place).astype(WIDE)
    for i in range(T // LANES):
        part = marks[:, i * LANES : (i + 1) * LANES]
        seg_col[i * LANES : (i + 1) * LANES, :] = jnp.broadcast_to(part, (LANES, LANES)).T

    def marks_of(i):
        there = seg_row[:, pl.ds(pl.multiple_of(i * BLOCK, BLOCK), BLOCK)]
        at = lax.broadcasted_iota(jnp.int32, (1, BLOCK), 1) + i * BLOCK
        return jnp.where(there >= 0, there, -1 - at).astype(WIDE)

    loop(nd - 1, lambda i: small(i + 1).wait_recv())

    low = lax.broadcasted_iota(jnp.int32, (LANES, F), 0) * nd
    col = lax.broadcasted_iota(jnp.int32, (LANES, F), 1)
    comb[...] = jnp.where((col >= low) & (col < low + nd), 1.0, 0.0).astype(NARROW)
    bias[...] = jnp.zeros_like(bias)

    def of_peer(i):
        return lax.broadcasted_iota(jnp.int32, (1, F), 1) % nd == i

    def spread(i):
        bias[...] += jnp.where(of_peer(i), dot(small_in[i].astype(NARROW), comb[...]), 0.0)

    loop(nd, spread)
    if cs == LANES:
        for i in range(nd):
            vec[0:8, i * cs : (i + 1) * cs] = small_in[i, 0:8, :]
    else:
        vec[...] = jnp.zeros_like(vec)

        def spread_vec(i):
            low = lax.broadcasted_iota(jnp.int32, (LANES, D), 0)
            col = lax.broadcasted_iota(jnp.int32, (LANES, D), 1)
            pick = jnp.where(col == i * cs + low, 1.0, 0.0).astype(NARROW)
            vec[...] += dot(small_in[i].astype(NARROW), pick)

        loop(nd, spread_vec)

    due("small")

    loads[3].wait()

    def norm_one(i):
        r = pl.ds(pl.multiple_of(i * 64, 64), 64)
        unit, _ = normalize(z1[r, :].astype(WIDE))
        z1[r, :] = (unit * vec[0:1, :] + vec[1:2, :]).astype(NARROW)

    quarter = T // 64 // 4

    def norm_quarter(j):
        lax.fori_loop(j * quarter, (j + 1) * quarter, lambda i, _: (norm_one(i), None)[1], None)

    for j in range(4):
        norm_quarter(j)
        due("norm" + str(j))

    loads[4].wait()

    def norm_own(i):
        r = pl.ds(pl.multiple_of(i * 64, 64), 64)
        unit, inverse = normalize(x_own[r, :].astype(WIDE))
        n1[r, :] = unit
        r1[r, :] = inverse

    loop(own // 64, norm_own)
    due("mine")

    loads[5].wait()
    loads[6].wait()

    def scale_cot(i):
        r = pl.ds(pl.multiple_of(i * 64, 64), 64)
        dm[r, :] = (dm[r, :].astype(WIDE) * vec[7:8, :]).astype(NARROW)

    loop(T // 64, scale_cot)
    ag_finish(HA)

    scaling = HEAD ** (-0.5)

    def project(p, i):
        r = pl.ds(pl.multiple_of(i * BLOCK, BLOCK), BLOCK)
        here = slice(p * half, (p + 1) * half)
        three = dot(z1[r, :], weights[p][0])
        query = (three[:, 0:half] + bias[8:9, here]).astype(NARROW)
        q[r, here] = (query.astype(WIDE) * scaling).astype(NARROW)
        key = three[:, half : 2 * half].astype(NARROW)
        k[r, here] = key
        value = (three[:, 2 * half :] + bias[9:10, here]).astype(NARROW)
        v[r, here] = value
        kt[here, r] = key.T
        vt[here, r] = value.T

    def head_rows(x, hh):
        parts = []
        if hh > 0:
            parts.append(jnp.zeros((hh * HEAD, x.shape[1]), x.dtype))
        parts.append(x[hh * HEAD : (hh + 1) * HEAD, :])
        if (hh + 1) * HEAD < x.shape[0]:
            parts.append(jnp.zeros((x.shape[0] - (hh + 1) * HEAD, x.shape[1]), x.dtype))
        return jnp.concatenate(parts, 0)

    def window(i):
        return pl.ds(pl.multiple_of((i // 2) * BLOCK, BLOCK), WINDOW)

    def part(i, c):
        return pl.ds(pl.multiple_of((i // 2) * BLOCK + c * LANES, LANES), LANES)

    parts = WINDOW // LANES
    mask = dk

    def score_place(hh, c):
        if hh % 2 == 0:
            return dv.at[c * LANES : (c + 1) * LANES, :]
        return m_acc.at[(c % 2) * LANES : (c % 2 + 1) * LANES, (c // 2) * BLOCK : (c // 2 + 1) * BLOCK]

    def attend(p, s):
        i = red_block(s)
        r = rows_of(i)
        w = window(i)
        here = marks_of(i)
        mine = slice(p * half, (p + 1) * half)
        for c in range(parts):
            keys = seg_col[part(i, c), :]
            keys = jnp.concatenate([keys, keys], 1)
            mask[c * LANES : (c + 1) * LANES, :] = jnp.where(keys == here, 0.0, NEGATIVE)
        qt = q[r, mine].T
        count = heads // 2
        highest, mixed = [None] * count, [None] * count

        def score(hh):
            queries = head_rows(qt, hh)
            top = None
            for c in range(parts):
                scores = dot(k[part(i, c), mine], queries) + mask[c * LANES : (c + 1) * LANES, :]
                score_place(hh, c)[...] = scores
                most = jnp.max(scores.reshape(LANES // 8, 8, BLOCK), 0)
                top = most if top is None else jnp.maximum(top, most)
            highest[hh] = jnp.max(top, 0, keepdims=True)

        def mix(hh):
            head = p * count + hh
            cols = slice(head * BLOCK, (head + 1) * BLOCK)
            total = jnp.zeros((8, BLOCK), WIDE)
            for c in range(parts):
                expo = jnp.exp(score_place(hh, c)[...] - highest[hh])
                total = total + fold(expo)
                probs[i, c * LANES : (c + 1) * LANES, cols] = expo.astype(NARROW)
            inverse = 1.0 / jnp.sum(total, 0, keepdims=True)
            inv[i, head : head + 1, :] = inverse
            mixed[hh] = dot(vt[head * HEAD : (head + 1) * HEAD, w], probs[i, :, cols]) * inverse

        score(0)
        for hh in range(1, count):
            score(hh)
            mix(hh - 1)
        mix(count - 1)
        mixed = jnp.concatenate(mixed, 0)
        ot[i, mine, :] = mixed
        o[r, mine] = mixed.astype(NARROW).T

    def project_two(p, j, place):
        lax.fori_loop(2 * j, 2 * j + 2, lambda i, _: (project(p, i), None)[1], None)
        due(place + str(j))

    def attend_one(s):
        attend(0, s)
        due_at("one", s)

    def attend_two(s):
        attend(1, s)

        @pl.when(s == 0)
        def _():
            ag_finish(MIX)

        acc[...] = dot_nt(o[rows_of(red_block(s)), :], w_mix[0])
        red_step(0, s)
        due_at("two", s)

    for j in range(2):
        project_two(0, j, "first")
    loop(nt, attend_one)
    ag_finish(HB)
    for j in range(2):
        project_two(1, j, "second")
    loop(nt, attend_two)

    def middle(i):
        r = pl.ds(pl.multiple_of(i * 64, 64), 64)
        a = red_rows(0, r) + vec[2:3, :]
        att[r, :] = a
        x = x_own[r, :].astype(WIDE) + vec[3:4, :] * a
        x1[r, :] = x
        unit, inverse = normalize(x)
        n2[r, :] = unit
        r2[r, :] = inverse
        row_own[r, :] = (unit * vec[4:5, :] + vec[5:6, :]).astype(NARROW)

    in_halves(0, 0, row_own, z2, middle)
    due("z2")
    ag_finish(EXP)

    def tile(n):
        return slice(n * BLOCK, (n + 1) * BLOCK)

    def in_tiles(count, product, act):
        product(0)
        for n in range(1, count):
            product(n)
            act(n - 1)
        act(count - 1)

    def gat_wait(g, src, ref, s):
        @pl.when(s == 1)
        def _():
            gat(g, src, ref, 0).wait_recv()

        @pl.when(s == 2)
        def _():
            gat_forward(g, src, ref)

        @pl.when(s == 3)
        def _():
            gat(g, src, ref, 1).wait_recv()

    def expand(s):
        gat_wait(0, row_own, z2, s)
        i = red_block(nt - 1 - s)
        r = rows_of(i)

        def product(n):
            acc[:, tile(n)] = dot(z2[r, :], w_exp[0, :, tile(n)])

        def act(n):
            for c in range(own // 32):
                there = pl.ds(pl.multiple_of(i * own + c * 32, 32), 32)
                value, rise = gelu_parts(acc[c * 32 : (c + 1) * 32, tile(n)] + bias[10:11, tile(n)])
                h[there, tile(n)] = value.astype(NARROW)
                slope[there, tile(n)] = rise.astype(NARROW)

        in_tiles(F // BLOCK, product, act)

        due_at("expand", s)

    loop(nt, expand)

    def grad_shrink(s):
        b = grad_order(s)
        cols = pl.ds(pl.multiple_of(b * BLOCK, BLOCK), BLOCK)
        g_shr[0, cols, :] = dot_tn(dm[:, cols], h[...]).astype(NARROW)
        grad_block_done(SHR, b)
        due_at("shrink", s)

    loop(blocks, grad_shrink)
    ag_finish(SHR)

    bias_sums[...] = jnp.zeros_like(bias_sums)
    sums[...] = jnp.zeros_like(sums)

    def back(s):
        i = red_block(s)
        r = rows_of(i)

        def product(n):
            acc[:, tile(n)] = dot(dm[r, :], w_shr[0, :, tile(n)])

        def act(n):
            total = jnp.zeros((8, BLOCK), WIDE)
            for c in range(own // 32):
                there = pl.ds(pl.multiple_of(i * own + c * 32, 32), 32)
                du = acc[c * 32 : (c + 1) * 32, tile(n)] * slope[there, tile(n)].astype(WIDE)
                du = du.astype(NARROW)
                slope[there, tile(n)] = du
                total = total + fold(du.astype(WIDE))
            bias_sums[16:24, tile(n)] += total

        in_tiles(F // BLOCK, product, act)
        for n in range(D // BLOCK):
            acc[:, tile(n)] = dot_nt(slope[r, :], w_exp[0, tile(n), :])
        red_step(0, s)

    loop(nt, back)

    def grad_expand(s):
        b = grad_order(s)
        cols = pl.ds(pl.multiple_of(b * BLOCK, BLOCK), BLOCK)
        g_exp[0, cols, :] = dot_tn(z2[:, cols], slope[...]).astype(NARROW)

        due_at("grow", s)

    loop(blocks, grad_expand)

    for j in range(4):
        gat(0, row_own, z2, j).wait_send()

    def middle_back(i):
        r = pl.ds(pl.multiple_of(i * 64, 64), 64)
        grad = red_rows(0, r)
        unit = n2[r, :]
        sums[4 * 8 : 5 * 8, :] += fold(grad * unit)
        sums[5 * 8 : 6 * 8, :] += fold(grad)
        dx1 = c_own[r, :].astype(WIDE) + norm_back(grad, vec[4:5, :], unit, r2[r, :])
        sums[3 * 8 : 4 * 8, :] += fold(dx1 * att[r, :])
        n2[r, :] = dx1
        grad_att = (vec[3:4, :] * dx1).astype(NARROW)
        row_own[r, :] = grad_att
        sums[2 * 8 : 3 * 8, :] += fold(grad_att.astype(WIDE))

    in_halves(0, 1, row_own, da, middle_back)

    def shrink(s):
        r = rows_of(red_block(s))
        m_acc[...] = dot_nt(h[r, :], w_shr[0])
        red_step(1, s)

    dk[...] = jnp.zeros_like(dk)
    dv[...] = jnp.zeros_like(dv)
    lane = lax.broadcasted_iota(jnp.int32, (1, C), 1)

    def grad_mix(s):
        b = grad_order(s)
        cols = pl.ds(pl.multiple_of(b * BLOCK, BLOCK), BLOCK)
        g_mix[0, cols, :] = dot_tn(da[:, cols], o[...]).astype(NARROW)
        grad_block_done(MIX, b)

    def attend_back(s):
        @pl.when(s == 2)
        def _():
            loop(nt, shrink)

        gat_wait(1, row_own, da, s)

        @pl.when(s == 2)
        def _():
            red(1, 2).start()
            red(1, 3).start()

        @pl.when(s == 3)
        def _():
            loop(blocks, grad_mix)

        i = red_block(nt - 1 - s)
        r = rows_of(i)
        w = window(i)
        do = dot(da[r, :], w_mix[0]).astype(NARROW)
        dot_ = do.T.astype(WIDE)
        whole = []
        for hh in range(heads):
            whole.append(jnp.broadcast_to(inv[i, hh : hh + 1, :], (HEAD, BLOCK)))
        scaled = dot_ * jnp.concatenate(whole, 0)
        delta = scaled * ot[i]
        scaled_t = scaled.astype(NARROW)
        natural = scaled_t.T.astype(WIDE)
        queries = q[r, :].astype(WIDE)
        back_q = []

        def grad_scores(hh):
            cols = slice(hh * BLOCK, (hh + 1) * BLOCK)
            here = (lane >= hh * HEAD) & (lane < (hh + 1) * HEAD)
            q_split[cols, :] = jnp.where(here, queries, 0.0).astype(NARROW)
            do_split[cols, :] = jnp.where(here, natural, 0.0).astype(NARROW)
            shift = jnp.sum(delta[hh * HEAD : (hh + 1) * HEAD, :], 0, keepdims=True)
            grads_o = head_rows(scaled_t, hh)
            for c in range(parts):
                place = slice(c * LANES, (c + 1) * LANES)
                grad_p = dot(v[part(i, c), :], grads_o)
                ds[place, cols] = (probs[i, place, cols].astype(WIDE) * (grad_p - shift)).astype(NARROW)

        def grad_queries(hh):
            cols = slice(hh * BLOCK, (hh + 1) * BLOCK)
            back_q.append(dot(kt[hh * HEAD : (hh + 1) * HEAD, w], ds[:, cols]))

        grad_scores(0)
        for hh in range(1, heads):
            grad_scores(hh)
            grad_queries(hh - 1)
        grad_queries(heads - 1)
        grad_q = (jnp.concatenate(back_q, 0) * scaling).astype(NARROW).T
        dqkv[r, 0:half] = grad_q[:, 0:half]
        dqkv[r, width : width + half] = grad_q[:, half:C]
        for c in range(WINDOW // BLOCK):
            place = slice(c * BLOCK, (c + 1) * BLOCK)
            there = pl.ds(pl.multiple_of((i // 2) * BLOCK + c * BLOCK, BLOCK), BLOCK)
            dk[there, :] += dot(ds[place, :], q_split[...])
            dv[there, :] += dot(probs[i, place, :], do_split[...])

        due_at("back", s)

    loop(nt, attend_back)

    def round_kv(i):
        r = pl.ds(pl.multiple_of(i * 128, 128), 128)
        grad_k = dk[r, :].astype(NARROW)
        grad_v = dv[r, :].astype(NARROW)
        for p in range(2):
            here = slice(p * half, (p + 1) * half)
            dqkv[r, p * width + half : p * width + 2 * half] = grad_k[:, here]
            dqkv[r, p * width + 2 * half : (p + 1) * width] = grad_v[:, here]
            bias_sums[0:8, here] += fold(dqkv[r, p * width : p * width + half].astype(WIDE))
        bias_sums[8:16, 0:C] += fold(grad_v.astype(WIDE))

    loop(T // 128, round_kv)

    def grad_qkv(s):
        b = grad_order(s)
        cols = pl.ds(pl.multiple_of(b * BLOCK, BLOCK), BLOCK)
        both = dot_tn(z1[:, cols], dqkv[...]).astype(NARROW)
        for p in range(2):
            grads[p][0, cols, :] = both[:, p * width : (p + 1) * width]
            grad_block_done(p, b)

    def first_back(s):
        r = rows_of(red_block(s))
        acc[...] = dot_nt(dqkv[r, 0:width], w_ha[0]) + dot_nt(dqkv[r, width : 2 * width], w_hb[0])
        red_step(0, s)

    loop(nt, first_back)
    loop(blocks, grad_qkv)
    due("heads")

    for j in range(4):
        gat(1, row_own, da, j).wait_send()

    def finish_y(i):
        r = pl.ds(pl.multiple_of(i * 64, 64), 64)
        m = red_rows(1, r) + vec[6:7, :]
        dy = c_own[r, :].astype(WIDE)
        sums[7 * 8 : 8 * 8, :] += fold(dy * m)
        sums[6 * 8 : 7 * 8, :] += fold((vec[7:8, :] * dy).astype(NARROW).astype(WIDE))
        row_own[r, :] = (x1[r, :] + vec[7:8, :] * m).astype(NARROW)

    in_halves(1, 2, row_own, dm, finish_y)

    due("y")
    def finish_dx(i):
        r = pl.ds(pl.multiple_of(i * 64, 64), 64)
        grad = red_rows(0, r)
        unit = n1[r, :]
        sums[0 * 8 : 1 * 8, :] += fold(grad * unit)
        sums[1 * 8 : 2 * 8, :] += fold(grad)
        dx = n2[r, :] + norm_back(grad, vec[0:1, :], unit, r1[r, :])
        x_own[r, :] = dx.astype(NARROW)

    in_halves(0, 3, x_own, z2, finish_dx)
    due("dx")

    for j in range(8):
        vec_parts[t, j : j + 1, :] = jnp.sum(sums[j * 8 : (j + 1) * 8, :], 0, keepdims=True)

    def vec_to(kk):
        return to_tensor(vec_parts.at[t], vec_parts.at[t], vs_s.at[kk], vs_r.at[kk], (t + kk) % nt)

    loop(nt - 1, lambda i: vec_to(i + 1).start())
    gat_forward(2, row_own, dm)
    loop(nt - 1, lambda i: vec_to(i + 1).wait_recv())
    total = vec_parts[0]
    for j in range(1, nt):
        total = total + vec_parts[j]
    lines = [jnp.sum(bias_sums[j * 8 : (j + 1) * 8, :], 0, keepdims=True) for j in range(3)]
    lines = jnp.concatenate(lines + [jnp.zeros((5, F), WIDE)], 0)
    high = lines.astype(NARROW).astype(WIDE)
    lines = jnp.concatenate([high, lines - high], 0)

    def pack(i):
        both = dot_nt(jnp.where(of_peer(i), lines, 0.0).astype(NARROW), comb[...])
        small_send[i, 8:16, :] = both[0:8, :] + both[8:16, :]

    loop(nd, pack)
    if cs == LANES:
        for i in range(nd):
            small_send[i, 0:8, :] = total[:, i * cs : (i + 1) * cs]
    else:
        vec_high = total.astype(NARROW)
        vec_low = (total - vec_high.astype(WIDE)).astype(NARROW)

        def pack_vec(i):
            row = lax.broadcasted_iota(jnp.int32, (D, LANES), 0)
            low = lax.broadcasted_iota(jnp.int32, (D, LANES), 1)
            pick = jnp.where((row == i * cs + low) & (low < cs), 1.0, 0.0).astype(NARROW)
            small_send[i, 0:8, :] = dot(vec_high, pick) + dot(vec_low, pick)

        loop(nd, pack_vec)

    def grad_small(kk):
        peer = (me + kk) % nd
        return to_dp(small_send.at[peer], small_recv.at[me], gs_s.at[kk], gs_r.at[kk], peer)

    loop(nd - 1, lambda i: grad_small(i + 1).start())
    small_recv[me] = small_send[me]
    due("pack")
    gat_forward(3, x_own, z2)
    due("last")
    loop(nd - 1, lambda i: grad_small(i + 1).wait_recv())
    out_small[...] = lax.fori_loop(
        1, nd, lambda i, s: s + small_recv[i], small_recv[0]
    )

    def ag_drain(a, d):
        for late in (False, True) if turned[a] else (False,):

            @pl.when((mz + 1 < no) & (mz + 1 >= d))
            def _():
                ag_right(a, d, late).wait_send()

            @pl.when((mz > 0) & (mz + d <= no))
            def _():
                ag_left(a, d, late).wait_send()

    keep = []
    for g, src, ref, out in ((2, row_own, dm, out_y), (3, x_own, z2, out_dx)):
        gat(g, src, ref, 0).wait_recv()
        gat(g, src, ref, 1).wait_recv()
        keep.append(load(8 + g, ref, out))
        keep[-1].start()
        for j in range(4):
            gat(g, src, ref, j).wait_send()
    for a in range(5):
        peers(functools.partial(ag_drain, a))
        ag_own(a).wait_send()
        peers(lambda i: ag_x(a, (mz + i) % no).wait_send())
        loop(no - 1, lambda i: rs_z(a, i + 1).wait_send())
        loop(no, lambda i: rs_x(a, i).wait_send())
    loop(nd - 1, lambda i: small(i + 1).wait_send())
    loop(nd - 1, lambda i: grad_small(i + 1).wait_send())
    loop(nt - 1, lambda i: vec_to(i + 1).wait_send())
    for copy in keep:
        copy.wait()


def layer(nd, nt, tokens, segments, cotangent, heads, mixer, expand, shrink, vector, biases, offset):
    T, D = tokens.shape
    C, F = heads.shape[2], expand.shape[1]
    cs, no, own = D // nd, nd // 2, T // nt
    sds = jax.ShapeDtypeStruct
    dma = pltpu.SemaphoreType.DMA

    def nar(*shape):
        return pltpu.VMEM(shape, NARROW)

    def wid(*shape):
        return pltpu.VMEM(shape, WIDE)

    shapes = ((1, 3 * C // 2), (1, 3 * C // 2), (1, C), (1, F), (1, F))
    scratch = [wid(*x.shape) for x in (mixer, shrink)]
    scratch += [nar(m, D, w) for m, w in shapes]
    scratch += [nar(T, D), nar(T, D), nar(own, D), nar(own, D), wid(T, LANES)]
    scratch += [wid(SMALL_ROWS, D), wid(SMALL_ROWS, F), wid(own, D), wid(own, 1)]
    scratch += [nar(T, C), nar(T, C), nar(T, C), nar(C, T), nar(C, T)]
    scratch += [nar(nt, WINDOW, (C // HEAD) * BLOCK)]
    scratch += [wid(nt, 8, BLOCK), wid(nt, C, BLOCK), nar(T, C), wid(own, D)]
    scratch += [wid(own, D), wid(own, D), wid(own, D), wid(own, 1)]
    scratch += [nar(T, D), nar(T, F), nar(T, F), nar(T, D)]
    scratch += [nar(WINDOW, (C // HEAD) * BLOCK), nar((C // HEAD) * BLOCK, C), nar((C // HEAD) * BLOCK, C)]
    scratch += [nar(T, 3 * C), wid(T, C), wid(T, C), nar(LANES, F)]
    scratch += [wid(64, D), wid(24, F), nar(own, D)]
    scratch += [nar(2, own, D), nar(2, own, D), nar(own, D), nar(own, D)]
    scratch += [wid(own, D), nar(2, own, D), nar(2, own, D), nar(own, D), nar(own, D)]
    scratch += [nar(m, D, w) for m, w in shapes]
    scratch += [nar(no, m, cs, w) for m, w in shapes]
    scratch += [nar(no - 1, m, cs, w) for m, w in shapes]
    scratch += [wid(nd, SMALL_ROWS, LANES), wid(nt, 8, D), wid(nd, SMALL_ROWS, LANES), wid(nd, SMALL_ROWS, LANES)]
    scratch += [dma((12,))]
    scratch += [dma((5, no + 1)) for _ in range(8)] + [dma((5, no)) for _ in range(6)]
    scratch += [dma((nd,)) for _ in range(4)]
    scratch += [dma((nt,)) for _ in range(2)]
    scratch += [dma((2, 4)), dma((2, 4)), dma((4, 4)), dma((4, 4))]

    anywhere = pl.BlockSpec(memory_space=pl.ANY)
    vmem = pl.BlockSpec(memory_space=pltpu.VMEM)
    return pl.pallas_call(
        functools.partial(kernel, nd, nt),
        out_shape=[
            sds((T, D), NARROW),
            sds((T, D), NARROW),
            *[sds((m, cs, w), WIDE) for m, w in shapes],
            sds((SMALL_ROWS, LANES), WIDE),
        ],
        in_specs=[anywhere, vmem] + [anywhere] * 5 + [vmem] * 3,
        out_specs=[anywhere, anywhere] + [vmem] * 6,
        scratch_shapes=scratch,
        compiler_params=pltpu.CompilerParams(
            collective_id=0, has_side_effects=True, vmem_limit_bytes=VMEM_LIMIT
        ),
    )(tokens, segments.reshape(1, T), cotangent, heads, mixer, expand, shrink, vector, biases, offset)


def update_kernel(*refs):
    raw_y, raw_dx = refs[:2]
    sources, refs = refs[2:29], refs[29:]
    out_y, out_dx = refs[:2]
    targets, refs = refs[2:16], refs[16:]
    held, news, t_mix, t_shr = refs[:27], refs[27:41], refs[41], refs[42]
    held_y, held_dx, sem = refs[43:]
    first = (0, 1, 6, 13, 20, 3, 9, 16, 23)
    loads = [pltpu.make_async_copy(sources[i], held[i], sem.at[i]) for i in range(27)]
    take = [
        pltpu.make_async_copy(raw_y, held_y, sem.at[27]),
        pltpu.make_async_copy(raw_dx, held_dx, sem.at[28]),
    ]
    for i in first:
        loads[i].start()
    for i in (4, 11, 18, 25, 2, 8, 15, 22):
        loads[i].start()
    for copy in take:
        copy.start()
    for i in (5, 7, 10, 12, 14, 17, 19, 21, 24, 26):
        loads[i].start()
    keep = [
        pltpu.make_async_copy(held_y, out_y, sem.at[43]),
        pltpu.make_async_copy(held_dx, out_dx, sem.at[44]),
    ]
    grads, state = held[:6], held[6:]
    stores = [pltpu.make_async_copy(news[i], targets[i], sem.at[29 + i]) for i in range(14)]

    def arrive(slot, source=None):
        if source is not None:
            loads[source].wait()
        for j in range(3):
            loads[6 + slot + 7 * j].wait()

    def update(slot, gradient, decay_rate, at=lambda ref: ref):
        master, moment, square = (at(state[slot + 7 * j])[...] for j in range(3))
        moment = BETA_ONE * moment + (1.0 - BETA_ONE) * gradient
        square = BETA_TWO * square + (1.0 - BETA_TWO) * gradient * gradient
        at(news[slot + 7])[...] = moment
        change = moment * (1 / CORRECT_ONE) / (jnp.sqrt(square * (1 / CORRECT_TWO)) + ADAM_EPS)
        at(news[slot])[...] = change + decay_rate * master

    def by_rows(slot, gradient, step):
        def one(c):
            r = pl.ds(pl.multiple_of(c * step, step), step)
            update(slot, gradient[r, :], WEIGHT_DECAY, lambda ref: ref.at[r, :])

        loop(gradient.shape[0] // step, one)

    def leave(slot):
        stores[slot].start()
        stores[slot + 7].start()

    loads[1].wait()
    arrive(0, 0)
    half = grads[0].shape[2] // 3
    for j in range(3):
        here = slice(j * half, (j + 1) * half)
        whole = jnp.concatenate([grads[0][0, :, here], grads[1][0, :, here]], 1)
        update(0, whole, WEIGHT_DECAY, lambda ref: ref.at[j])
    leave(0)
    arrive(3, 3)
    by_rows(3, grads[3].at[0], min(32, grads[3].shape[1]))
    leave(3)
    for j in range(2):
        take[j].wait()
        keep[j].start()
    arrive(5, 4)
    t_shr[...] = grads[4][0].T
    by_rows(5, t_shr, 256)
    leave(5)
    arrive(2, 2)
    t_mix[...] = grads[2][0].T
    by_rows(2, t_mix, 256)
    leave(2)
    loads[5].wait()
    small = grads[5]
    for slot, rows in ((1, slice(8, 10)), (4, slice(10, 11)), (6, slice(0, 8))):
        arrive(slot)
        update(slot, small[rows, 0 : state[slot].shape[1]], 0.0)
        leave(slot)
    for copy in keep + stores:
        copy.wait()


def shards(nd, nt, tokens, segments, cotangent, *state):
    heads, biases, mixer, expand, offset, shrink, vector = state[:7]
    flat = list(state)
    for j in range(0, 21, 7):
        flat[j + 1] = state[j + 1].reshape(2, -1)
        flat[j + 4] = state[j + 4].reshape(1, -1)
    results = layer(nd, nt, tokens, segments, cotangent, heads, mixer, expand, shrink, vector, flat[1], flat[4])
    anywhere = pl.BlockSpec(memory_space=pl.ANY)
    sds = jax.ShapeDtypeStruct
    outs = pl.pallas_call(
        update_kernel,
        out_shape=[sds(x.shape, x.dtype) for x in results[:2]] + [sds(x.shape, WIDE) for x in flat[:7]] * 2,
        in_specs=[anywhere] * 29,
        out_specs=[anywhere] * 16,
        scratch_shapes=[
            *[pltpu.VMEM(x.shape, WIDE) for x in (*results[2:], *flat, *flat[:7], *flat[:7], mixer, shrink)],
            pltpu.VMEM(results[0].shape, NARROW),
            pltpu.VMEM(results[1].shape, NARROW),
            pltpu.SemaphoreType.DMA((45,)),
        ],
        compiler_params=pltpu.CompilerParams(vmem_limit_bytes=VMEM_LIMIT),
    )(*results, *flat)
    outs = list(outs)
    for j in (2, 9):
        outs[j + 1] = outs[j + 1].reshape(biases.shape)
        outs[j + 4] = outs[j + 4].reshape(offset.shape)
    return tuple(outs)


def solution(mesh):
    matrices = (
        P(None, "dp", "tensor"),
        P(None, "tensor", "dp"),
        P("tensor", "dp"),
        P("dp", "tensor"),
        P("tensor", "dp"),
        P("tensor", "dp"),
        P(None, "dp"),
    )
    rows = P("dp", None)
    return jax.shard_map(
        functools.partial(shards, mesh.shape["dp"], mesh.shape["tensor"]),
        mesh=mesh,
        in_specs=(rows, P("dp"), rows) + matrices * 3,
        out_specs=(rows, rows) + matrices * 2,
        check_vma=False,
    )
```

```python
import functools

import jax
import jax.numpy as jnp
from jax import lax
from jax.experimental import pallas as pl
from jax.experimental.pallas import tpu as pltpu
from jax.sharding import PartitionSpec as P

MESH = pl.DeviceIdType.MESH
WIDE, NARROW = jnp.float32, jnp.bfloat16

HEAD = 64
BLOCK = 256
WINDOW = 768
SMALL_ROWS = 16
VMEM_LIMIT = 66 * 1024 * 1024
LANES = 128

NORM_EPS = 1e-06
NEGATIVE = -1e30
INV_ROOT_TAU = 0.3989422804014327
BETA_ONE = 0.9
BETA_TWO = 0.999
ADAM_EPS = 1e-08
WEIGHT_DECAY = 0.05
CORRECT_ONE = 0.9999734386011124
CORRECT_TWO = 0.0952078528862904

HA, HB, MIX, EXP, SHR = 0, 1, 2, 3, 4

PLAN = {
    "start": [("begin", HB)],
    "cast": [("own", EXP)],
    "small": [("step", HA, 1)],
    "norm0": [("begin", MIX)],
    "norm1": [("step", HA, 2)],
    "norm2": [("step", HB, 1), ("step", MIX, 1)],
    "norm3": [("step", HA, 3), ("begin", EXP), ("step", HB, 2)],
    "mine": [("own", HB)],
    "first0": [("step", MIX, 2)],
    "one0": [("step", HB, 3)],
    "one1": [("own", MIX), ("step", MIX, 3), ("step", EXP, 1)],
    "one2": [("turn", EXP)],
    "two0": [("begin", SHR)],
    "two1": [("own", SHR), ("step", EXP, 2), ("late", EXP, 1)],
    "two2": [("step", EXP, 3), ("step", SHR, 1)],
    "two3": [("late", EXP, 2), ("turn", SHR)],
    "z2": [("late", EXP, 3), ("step", SHR, 2)],
    "expand1": [("late", SHR, 1), ("step", SHR, 3)],
    "expand2": [("late", SHR, 2)],
    "shrink2": [("late", SHR, 3)],
    "grow0": [("on", SHR, 1)],
    "grow2": [("leave", EXP, 0)],
    "grow3": [("on", SHR, 2)],
    "back0": [("on", SHR, 3), ("leave", EXP, 1), ("leave", EXP, 2)],
    "back1": [("leave", EXP, 3)],
    "back2": [("on", EXP, 1)],
    "back3": [("on", EXP, 2)],
    "heads": [("on", EXP, 3), ("on", MIX, 1), ("on", MIX, 2)],
    "y": [("on", MIX, 3), ("on", HA, 1), ("on", HB, 1), ("on", HA, 2), ("on", HB, 2)],
    "dx": [("on", HA, 3), ("on", HB, 3)],
    "pack": [("end", SHR), ("end", EXP)],
    "last": [("end", MIX), ("end", HA), ("end", HB)],
}


def dot(a, b):
    return jnp.dot(a, b, preferred_element_type=WIDE)


def dot_nt(a, b):
    return lax.dot_general(a, b, (((1,), (1,)), ((), ())), preferred_element_type=WIDE)


def dot_tn(a, b):
    return lax.dot_general(a, b, (((0,), (0,)), ((), ())), preferred_element_type=WIDE)


def loop(count, body):
    lax.fori_loop(0, count, lambda i, _: (body(i), None)[1], None)


def normalize(stream):
    center = stream - jnp.mean(stream, -1, keepdims=True)
    inverse = lax.rsqrt(jnp.mean(center * center, -1, keepdims=True) + NORM_EPS)
    return center * inverse, inverse


def norm_back(grad, gain, unit, inverse):
    scaled = grad * gain
    return inverse * (
        scaled - jnp.mean(scaled, -1, keepdims=True) - unit * jnp.mean(scaled * unit, -1, keepdims=True)
    )


def gelu_parts(u):
    bell = jnp.exp(-0.5 * u * u)
    base = 1.0 + (0.3275911 * 0.7071067811865476) * jnp.abs(u)
    t = pl.reciprocal(base, approx=True)
    t = t * (2.0 - base * t)
    poly = t * (
        0.5 * 0.254829592
        + t * (-0.5 * 0.284496736 + t * (0.5 * 1.421413741 + t * (-0.5 * 1.453152027 + t * (0.5 * 1.061405429))))
    )
    tail = poly * bell
    cdf = jnp.where(u >= 0, 1.0 - tail, tail)
    return u * cdf, cdf + u * bell * INV_ROOT_TAU


def fold(x):
    return jnp.sum(x.reshape(x.shape[0] // 8, 8, x.shape[1]), 0)


def kernel(
    nd,
    nt,
    tokens,
    seg_row,
    cotangent,
    own_qkv,
    own_mix,
    own_exp,
    own_shr,
    own_vec,
    own_bias,
    own_off,
    out_y,
    out_dx,
    out_ha,
    out_hb,
    out_mix,
    out_exp,
    out_shr,
    out_small,
    l_mix,
    l_shr,
    w_ha,
    w_hb,
    w_mix,
    w_exp,
    w_shr,
    z1,
    dm,
    x_own,
    c_own,
    seg_col,
    vec,
    bias,
    n1,
    r1,
    q,
    k,
    v,
    kt,
    vt,
    probs,
    inv,
    ot,
    o,
    acc,
    x1,
    att,
    n2,
    r2,
    z2,
    h,
    slope,
    da,
    ds,
    q_split,
    do_split,
    dqkv,
    dk,
    dv,
    comb,
    sums,
    bias_sums,
    row_own,
    sb,
    rb1,
    s2,
    rb2,
    m_acc,
    m_sb,
    m_rb1,
    m_s2,
    m_rb2,
    g_ha,
    g_hb,
    g_mix,
    g_exp,
    g_shr,
    p_ha,
    p_hb,
    p_mix,
    p_exp,
    p_shr,
    f_ha,
    f_hb,
    f_mix,
    f_exp,
    f_shr,
    small_in,
    vec_parts,
    small_send,
    small_recv,
    local_sem,
    ag_rs,
    ag_rr,
    ag_ls,
    ag_lr,
    ag_brs,
    ag_brr,
    ag_bls,
    ag_blr,
    ag_xs,
    ag_xr,
    rs_zs,
    rs_zr,
    rs_xs,
    rs_xr,
    sm_s,
    sm_r,
    gs_s,
    gs_r,
    vs_s,
    vs_r,
    red_s,
    red_r,
    gat_s,
    gat_r,
):
    T, D = z1.shape
    C = q.shape[1]
    F = h.shape[1]
    no = nd // 2
    cs = D // nd
    heads = C // HEAD
    blocks = D // BLOCK
    pairs = BLOCK // (2 * cs)
    own = T // nt

    me = lax.axis_index("dp")
    t = lax.axis_index("tensor")
    mz = me // 2
    mx = me % 2
    x_peer = me + 1 - 2 * mx
    mate = t + 1 - 2 * (t % 2)
    cross = (t + 2) % nt
    far = mate + 2 - 4 * (mate // 2)

    weights = (w_ha, w_hb, w_mix, w_exp, w_shr)
    grads = (g_ha, g_hb, g_mix, g_exp, g_shr)
    firsts = (p_ha, p_hb, p_mix, p_exp, p_shr)
    seconds = (f_ha, f_hb, f_mix, f_exp, f_shr)
    finals = (out_ha, out_hb, out_mix, out_exp, out_shr)
    half = C // 2
    width = 3 * half

    def rows_of(i):
        return pl.ds(pl.multiple_of(i * own, own), own)

    def chunk(ref, i):
        return ref.at[:, pl.ds(pl.multiple_of(i * cs, cs), cs), :]

    def to_dp(src, dst, send, recv, peer):
        return pltpu.make_async_remote_copy(
            src_ref=src, dst_ref=dst, send_sem=send, recv_sem=recv, device_id={"dp": peer}, device_id_type=MESH
        )

    def to_tensor(src, dst, send, recv, peer):
        return pltpu.make_async_remote_copy(
            src_ref=src, dst_ref=dst, send_sem=send, recv_sem=recv, device_id={"tensor": peer}, device_id_type=MESH
        )

    def load(i, src, dst):
        return pltpu.make_async_copy(src, dst, local_sem.at[i])

    loads = [
        load(0, own_mix, l_mix),
        load(1, own_exp, x1.at[0:cs, :]),
        load(2, own_shr, l_shr),
        load(3, tokens, z1),
        load(4, tokens.at[rows_of(t), :], x_own),
        load(5, cotangent, dm),
        load(6, cotangent.at[rows_of(t), :], c_own),
        *[load(7 + j, own_qkv.at[j], att.at[0:cs, j * C : (j + 1) * C]) for j in range(3)],
    ]
    for copy in loads[7:] + loads[:7]:
        copy.start()

    barrier = pltpu.get_barrier_semaphore()

    def greet_dp(i):
        pl.semaphore_signal(barrier, inc=1, device_id={"dp": (me + 1 + i) % nd}, device_id_type=MESH)

    def greet_tensor(i):
        pl.semaphore_signal(barrier, inc=1, device_id={"tensor": (t + 1 + i) % nt}, device_id_type=MESH)

    loop(nd - 1, greet_dp)
    loop(nt - 1, greet_tensor)

    small_in[me] = jnp.zeros_like(small_in[me])
    small_in[me, 0:8, 0:cs] = own_vec[...].astype(NARROW).astype(WIDE)
    small_in[me, 8:10, 0 : own_bias.shape[1]] = own_bias[...].astype(NARROW).astype(WIDE)
    small_in[me, 10:11, 0 : own_off.shape[1]] = own_off[...].astype(NARROW).astype(WIDE)
    for copy in loads[7:]:
        copy.wait()
    mine = pl.ds(pl.multiple_of(me * cs, cs), cs)
    for p in range(2):
        for j in range(3):
            own_part = att[0:cs, j * C + p * half : j * C + (p + 1) * half]
            weights[p][0, mine, j * half : (j + 1) * half] = own_part.astype(NARROW)
    loads[0].wait()
    w_mix[0, mine, :] = l_mix[...].T.astype(NARROW)

    pl.semaphore_wait(barrier, nd + nt - 2)

    turned = (0, 0, 0, F // 4, F // 4)

    def columns(a, i, late):
        width = weights[a].shape[2]
        split = width - turned[a]
        lanes = pl.ds(split, turned[a]) if late else pl.ds(0, split)
        return weights[a].at[:, pl.ds(pl.multiple_of(i * cs, cs), cs), lanes]

    def ag_own(a):
        slot = chunk(weights[a], me)
        return to_dp(slot, slot, ag_xs.at[a, mz], ag_xr.at[a, mz], x_peer)

    def ag_x(a, source):
        slot = columns(a, source * 2 + mx, False)
        return to_dp(slot, slot, ag_xs.at[a, source], ag_xr.at[a, source], x_peer)

    def ag_right(a, d, late=False):
        source = (mz + no + 1 - d) % no
        slot = columns(a, source * 2 + 1 - mx, True) if late else chunk(weights[a], source * 2 + mx)
        send, recv = (ag_brs, ag_brr) if late else (ag_rs, ag_rr)
        return to_dp(slot, slot, send.at[a, d], recv.at[a, d], ((mz + 1) % no) * 2 + mx)

    def ag_left(a, d, late=False):
        source = (mz + d - 1) % no
        slot = columns(a, source * 2 + 1 - mx, True) if late else chunk(weights[a], source * 2 + mx)
        send, recv = (ag_bls, ag_blr) if late else (ag_ls, ag_lr)
        return to_dp(slot, slot, send.at[a, d], recv.at[a, d], ((mz + no - 1) % no) * 2 + mx)

    def ag_leave(a, late):
        @pl.when(mz + 1 < no)
        def _():
            ag_right(a, 1, late).start()

        @pl.when(mz > 0)
        def _():
            ag_left(a, 1, late).start()

    def ag_begin(a):
        ag_leave(a, False)

    def ag_turn(a):
        ag_own(a).wait_recv()
        ag_leave(a, True)

    def ag_step(a, d, late=False):
        @pl.when(mz >= d)
        def _():
            ag_right(a, d, late).wait_recv()

            @pl.when(mz + 1 < no)
            def _():
                ag_right(a, d + 1, late).start()

            if not late:
                ag_x(a, mz - d).start()

        @pl.when(mz + d < no)
        def _():
            ag_left(a, d, late).wait_recv()

            @pl.when(mz > 0)
            def _():
                ag_left(a, d + 1, late).start()

            if not late:
                ag_x(a, mz + d).start()

    def thirds(j, body):
        low, high = 1 + (j - 1) * (no - 1) // 3, 1 + j * (no - 1) // 3
        lax.fori_loop(low, high, lambda i, _: (body(i), None)[1], None)

    def ag_third(a, j, late=False):
        if turned[a] or not late:
            thirds(j, lambda d: ag_step(a, d, late))

    def ag_finish(a):
        if not turned[a]:
            ag_own(a).wait_recv()
        peers(lambda i: ag_x(a, (mz + i) % no).wait_recv())

    def peers(body):
        loop(no - 1, lambda i: body(i + 1))

    def rs_x(a, zz):
        return to_dp(
            chunk(grads[a], zz * 2 + 1 - mx), firsts[a].at[zz], rs_xs.at[a, zz], rs_xr.at[a, zz], x_peer
        )

    def rs_z(a, kk):
        zz = (mz + kk) % no
        return to_dp(firsts[a].at[zz], seconds[a].at[kk - 1], rs_zs.at[a, kk], rs_zr.at[a, kk], zz * 2 + mx)

    def add_step(width):
        return min(cs, 128 if width <= 256 else 32)

    def rs_forward(a, kk):
        zz = (mz + kk) % no
        rs_x(a, zz).wait_recv()
        here = chunk(grads[a], zz * 2 + mx)
        step = add_step(here.shape[2])

        def add(c):
            r = pl.ds(pl.multiple_of(c * step, step), step)
            total = here[0, r, :].astype(WIDE) + firsts[a][zz, 0, r, :].astype(WIDE)
            firsts[a][zz, 0, r, :] = total.astype(NARROW)

        loop(cs // step, add)
        rs_z(a, kk).start()

    def rs_third(a, j):
        thirds(j, lambda kk: rs_forward(a, kk))

    def rs_finish(a):
        rs_x(a, mz).wait_recv()
        loop(no - 1, lambda i: rs_z(a, i + 1).wait_recv())
        here = chunk(grads[a], me)
        step = add_step(here.shape[2])

        def add(c):
            r = pl.ds(pl.multiple_of(c * step, step), step)
            total = here[0, r, :].astype(WIDE) + firsts[a][mz, 0, r, :].astype(WIDE)
            if no <= 4:
                for kk in range(no - 1):
                    total = total + seconds[a][kk, 0, r, :].astype(WIDE)
            else:
                total = lax.fori_loop(
                    0, no - 1, lambda kk, partial: partial + seconds[a][kk, 0, r, :].astype(WIDE), total
                )
            finals[a][0, r, :] = total

        loop(cs // step, add)

    def grad_block_done(a, b):
        loop(pairs, lambda j: rs_x(a, b * pairs + j).start())

    def grad_order(s):
        return (mz // pairs + 1 + s) % blocks

    steps = {
        "begin": ag_begin,
        "own": lambda a: ag_own(a).start(),
        "step": ag_third,
        "turn": ag_turn,
        "late": lambda a, j: ag_third(a, j, True),
        "leave": lambda a, j: grad_block_done(a, grad_order(j)),
        "on": rs_third,
        "end": rs_finish,
    }

    def due(place):
        for name, *args in PLAN.get(place, ()):
            steps[name](*args)

    def due_at(place, s):
        for j in range(nt):
            if place + str(j) in PLAN:

                @pl.when(s == j)
                def _():
                    due(place + str(j))

    bufs = ((sb, rb1, s2, rb2, acc), (m_sb, m_rb1, m_s2, m_rb2, m_acc))

    part_rows = own // 2

    def red(c, j):
        send, first, pair, second, _ = bufs[c]
        if j >= 2:
            rows = slice((j - 2) * part_rows, (j - 1) * part_rows)
            return to_tensor(pair.at[rows, :], second.at[rows, :], red_s.at[c, j], red_r.at[c, j], cross)
        return to_tensor(send.at[j], first.at[j], red_s.at[c, j], red_r.at[c, j], mate)

    def red_block(s):
        second = (s % 2) * 1
        first_half = far + (cross - far) * second
        last_half = mate + (t - mate) * second
        return first_half + (last_half - first_half) * (s // 2)

    def red_step(c, s):
        send, first, pair, _, total = bufs[c]

        @pl.when(s == 0)
        def _():
            send[0] = total[...].astype(NARROW)
            red(c, 0).start()

        @pl.when(s == 1)
        def _():
            red(c, 0).wait_recv()
            for hh in range(2):
                rows = slice(hh * part_rows, (hh + 1) * part_rows)
                pair[rows, :] = (total[rows, :] + first[0, rows, :].astype(WIDE)).astype(NARROW)
                if c == 0:
                    red(c, 2 + hh).start()

        @pl.when(s == 2)
        def _():
            send[1] = total[...].astype(NARROW)
            red(c, 1).start()

    def red_wait(c, hh):
        if hh == 0:
            red(c, 1).wait_recv()
        red(c, 2 + hh).wait_recv()

    def red_drain(c):
        for j in range(4):
            red(c, j).wait_send()

    def red_rows(c, r):
        _, first, _, second, total = bufs[c]
        return total[r, :] + first[1, r, :].astype(WIDE) + second[r, :].astype(WIDE)

    def gat(g, src, ref, j):
        if j == 0:
            return to_tensor(src, ref.at[rows_of(t), :], gat_s.at[g, 0], gat_r.at[g, 0], mate)
        if j == 1:
            block = ref.at[rows_of(cross), :]
            return to_tensor(block, block, gat_s.at[g, 1], gat_r.at[g, 1], mate)
        rows = slice((j - 2) * part_rows, (j - 1) * part_rows)
        there = pl.ds(pl.multiple_of(t * own + (j - 2) * part_rows, part_rows), part_rows)
        return to_tensor(src.at[rows, :], ref.at[there, :], gat_s.at[g, j], gat_r.at[g, j], cross)

    def in_halves(c, g, src, ref, body):
        steps = own // 64 // 2
        for hh in range(2):
            red_wait(c, hh)
            lax.fori_loop(hh * steps, (hh + 1) * steps, lambda i, _: (body(i), None)[1], None)
            gat(g, src, ref, 2 + hh).start()
        gat(g, src, ref, 0).start()
        ref[rows_of(t), :] = src[...]
        red_drain(c)

    def gat_forward(g, src, ref):
        for hh in range(2):
            gat(g, src, ref, 2 + hh).wait_recv()
        gat(g, src, ref, 1).start()

    def small(kk):
        return to_dp(small_in.at[me], small_in.at[me], sm_s.at[kk], sm_r.at[kk], (me + kk) % nd)

    loop(nd - 1, lambda i: small(i + 1).start())
    ag_begin(HA)
    ag_own(HA).start()
    due("start")
    loads[1].wait()
    w_exp[0, mine, :] = x1[0:cs, :].astype(NARROW)
    loads[2].wait()
    w_shr[0, mine, :] = l_shr[...].T.astype(NARROW)
    due("cast")

    place = lax.broadcasted_iota(jnp.int32, (1, T), 1)
    marks = seg_row[...]
    marks = jnp.where(marks >= 0, marks, -1 - place).astype(WIDE)
    for i in range(T // LANES):
        part = marks[:, i * LANES : (i + 1) * LANES]
        seg_col[i * LANES : (i + 1) * LANES, :] = jnp.broadcast_to(part, (LANES, LANES)).T

    def marks_of(i):
        there = seg_row[:, pl.ds(pl.multiple_of(i * BLOCK, BLOCK), BLOCK)]
        at = lax.broadcasted_iota(jnp.int32, (1, BLOCK), 1) + i * BLOCK
        return jnp.where(there >= 0, there, -1 - at).astype(WIDE)

    loop(nd - 1, lambda i: small(i + 1).wait_recv())

    low = lax.broadcasted_iota(jnp.int32, (LANES, F), 0) * nd
    col = lax.broadcasted_iota(jnp.int32, (LANES, F), 1)
    comb[...] = jnp.where((col >= low) & (col < low + nd), 1.0, 0.0).astype(NARROW)
    bias[...] = jnp.zeros_like(bias)

    def of_peer(i):
        return lax.broadcasted_iota(jnp.int32, (1, F), 1) % nd == i

    def spread(i):
        bias[...] += jnp.where(of_peer(i), dot(small_in[i].astype(NARROW), comb[...]), 0.0)

    loop(nd, spread)
    if cs == LANES:
        for i in range(nd):
            vec[0:8, i * cs : (i + 1) * cs] = small_in[i, 0:8, :]
    else:
        vec[...] = jnp.zeros_like(vec)

        def spread_vec(i):
            low = lax.broadcasted_iota(jnp.int32, (LANES, D), 0)
            col = lax.broadcasted_iota(jnp.int32, (LANES, D), 1)
            pick = jnp.where(col == i * cs + low, 1.0, 0.0).astype(NARROW)
            vec[...] += dot(small_in[i].astype(NARROW), pick)

        loop(nd, spread_vec)

    due("small")

    loads[3].wait()

    def norm_one(i):
        r = pl.ds(pl.multiple_of(i * 64, 64), 64)
        unit, _ = normalize(z1[r, :].astype(WIDE))
        z1[r, :] = (unit * vec[0:1, :] + vec[1:2, :]).astype(NARROW)

    quarter = T // 64 // 4

    def norm_quarter(j):
        lax.fori_loop(j * quarter, (j + 1) * quarter, lambda i, _: (norm_one(i), None)[1], None)

    for j in range(4):
        norm_quarter(j)
        due("norm" + str(j))

    loads[4].wait()

    def norm_own(i):
        r = pl.ds(pl.multiple_of(i * 64, 64), 64)
        unit, inverse = normalize(x_own[r, :].astype(WIDE))
        n1[r, :] = unit
        r1[r, :] = inverse

    loop(own // 64, norm_own)
    due("mine")

    loads[5].wait()
    loads[6].wait()

    def scale_cot(i):
        r = pl.ds(pl.multiple_of(i * 64, 64), 64)
        dm[r, :] = (dm[r, :].astype(WIDE) * vec[7:8, :]).astype(NARROW)

    loop(T // 64, scale_cot)
    ag_finish(HA)

    scaling = HEAD ** (-0.5)

    def project(p, i):
        r = pl.ds(pl.multiple_of(i * BLOCK, BLOCK), BLOCK)
        here = slice(p * half, (p + 1) * half)
        three = dot(z1[r, :], weights[p][0])
        query = (three[:, 0:half] + bias[8:9, here]).astype(NARROW)
        q[r, here] = (query.astype(WIDE) * scaling).astype(NARROW)
        key = three[:, half : 2 * half].astype(NARROW)
        k[r, here] = key
        value = (three[:, 2 * half :] + bias[9:10, here]).astype(NARROW)
        v[r, here] = value
        kt[here, r] = key.T
        vt[here, r] = value.T

    def head_rows(x, hh):
        parts = []
        if hh > 0:
            parts.append(jnp.zeros((hh * HEAD, x.shape[1]), x.dtype))
        parts.append(x[hh * HEAD : (hh + 1) * HEAD, :])
        if (hh + 1) * HEAD < x.shape[0]:
            parts.append(jnp.zeros((x.shape[0] - (hh + 1) * HEAD, x.shape[1]), x.dtype))
        return jnp.concatenate(parts, 0)

    def window(i):
        return pl.ds(pl.multiple_of((i // 2) * BLOCK, BLOCK), WINDOW)

    def part(i, c):
        return pl.ds(pl.multiple_of((i // 2) * BLOCK + c * LANES, LANES), LANES)

    parts = WINDOW // LANES
    mask = dk

    def score_place(hh, c):
        if hh % 2 == 0:
            return dv.at[c * LANES : (c + 1) * LANES, :]
        return m_acc.at[(c % 2) * LANES : (c % 2 + 1) * LANES, (c // 2) * BLOCK : (c // 2 + 1) * BLOCK]

    def attend(p, s):
        i = red_block(s)
        r = rows_of(i)
        w = window(i)
        here = marks_of(i)
        mine = slice(p * half, (p + 1) * half)
        for c in range(parts):
            keys = seg_col[part(i, c), :]
            keys = jnp.concatenate([keys, keys], 1)
            mask[c * LANES : (c + 1) * LANES, :] = jnp.where(keys == here, 0.0, NEGATIVE)
        qt = q[r, mine].T
        count = heads // 2
        highest, mixed = [None] * count, [None] * count

        def score(hh):
            queries = head_rows(qt, hh)
            top = None
            for c in range(parts):
                scores = dot(k[part(i, c), mine], queries) + mask[c * LANES : (c + 1) * LANES, :]
                score_place(hh, c)[...] = scores
                most = jnp.max(scores.reshape(LANES // 8, 8, BLOCK), 0)
                top = most if top is None else jnp.maximum(top, most)
            highest[hh] = jnp.max(top, 0, keepdims=True)

        def mix(hh):
            head = p * count + hh
            cols = slice(head * BLOCK, (head + 1) * BLOCK)
            total = jnp.zeros((8, BLOCK), WIDE)
            for c in range(parts):
                expo = jnp.exp(score_place(hh, c)[...] - highest[hh])
                total = total + fold(expo)
                probs[i, c * LANES : (c + 1) * LANES, cols] = expo.astype(NARROW)
            inverse = 1.0 / jnp.sum(total, 0, keepdims=True)
            inv[i, head : head + 1, :] = inverse
            mixed[hh] = dot(vt[head * HEAD : (head + 1) * HEAD, w], probs[i, :, cols]) * inverse

        score(0)
        for hh in range(1, count):
            score(hh)
            mix(hh - 1)
        mix(count - 1)
        mixed = jnp.concatenate(mixed, 0)
        ot[i, mine, :] = mixed
        o[r, mine] = mixed.astype(NARROW).T

    def project_two(p, j, place):
        lax.fori_loop(2 * j, 2 * j + 2, lambda i, _: (project(p, i), None)[1], None)
        due(place + str(j))

    def attend_one(s):
        attend(0, s)
        due_at("one", s)

    def attend_two(s):
        attend(1, s)

        @pl.when(s == 0)
        def _():
            ag_finish(MIX)

        acc[...] = dot_nt(o[rows_of(red_block(s)), :], w_mix[0])
        red_step(0, s)
        due_at("two", s)

    for j in range(2):
        project_two(0, j, "first")
    loop(nt, attend_one)
    ag_finish(HB)
    for j in range(2):
        project_two(1, j, "second")
    loop(nt, attend_two)

    def middle(i):
        r = pl.ds(pl.multiple_of(i * 64, 64), 64)
        a = red_rows(0, r) + vec[2:3, :]
        att[r, :] = a
        x = x_own[r, :].astype(WIDE) + vec[3:4, :] * a
        x1[r, :] = x
        unit, inverse = normalize(x)
        n2[r, :] = unit
        r2[r, :] = inverse
        row_own[r, :] = (unit * vec[4:5, :] + vec[5:6, :]).astype(NARROW)

    in_halves(0, 0, row_own, z2, middle)
    due("z2")
    ag_finish(EXP)

    def tile(n):
        return slice(n * BLOCK, (n + 1) * BLOCK)

    def in_tiles(count, product, act):
        product(0)
        for n in range(1, count):
            product(n)
            act(n - 1)
        act(count - 1)

    def gat_wait(g, src, ref, s):
        @pl.when(s == 1)
        def _():
            gat(g, src, ref, 0).wait_recv()

        @pl.when(s == 2)
        def _():
            gat_forward(g, src, ref)

        @pl.when(s == 3)
        def _():
            gat(g, src, ref, 1).wait_recv()

    def expand(s):
        gat_wait(0, row_own, z2, s)
        i = red_block(nt - 1 - s)
        r = rows_of(i)

        def product(n):
            acc[:, tile(n)] = dot(z2[r, :], w_exp[0, :, tile(n)])

        def act(n):
            for c in range(own // 32):
                there = pl.ds(pl.multiple_of(i * own + c * 32, 32), 32)
                value, rise = gelu_parts(acc[c * 32 : (c + 1) * 32, tile(n)] + bias[10:11, tile(n)])
                h[there, tile(n)] = value.astype(NARROW)
                slope[there, tile(n)] = rise.astype(NARROW)

        in_tiles(F // BLOCK, product, act)

        due_at("expand", s)

    loop(nt, expand)

    def grad_shrink(s):
        b = grad_order(s)
        cols = pl.ds(pl.multiple_of(b * BLOCK, BLOCK), BLOCK)
        g_shr[0, cols, :] = dot_tn(dm[:, cols], h[...]).astype(NARROW)
        grad_block_done(SHR, b)
        due_at("shrink", s)

    loop(blocks, grad_shrink)
    ag_finish(SHR)

    bias_sums[...] = jnp.zeros_like(bias_sums)
    sums[...] = jnp.zeros_like(sums)

    def back(s):
        i = red_block(s)
        r = rows_of(i)

        def product(n):
            acc[:, tile(n)] = dot(dm[r, :], w_shr[0, :, tile(n)])

        def act(n):
            total = jnp.zeros((8, BLOCK), WIDE)
            for c in range(own // 32):
                there = pl.ds(pl.multiple_of(i * own + c * 32, 32), 32)
                du = acc[c * 32 : (c + 1) * 32, tile(n)] * slope[there, tile(n)].astype(WIDE)
                du = du.astype(NARROW)
                slope[there, tile(n)] = du
                total = total + fold(du.astype(WIDE))
            bias_sums[16:24, tile(n)] += total

        in_tiles(F // BLOCK, product, act)
        for n in range(D // BLOCK):
            acc[:, tile(n)] = dot_nt(slope[r, :], w_exp[0, tile(n), :])
        red_step(0, s)

    loop(nt, back)

    def grad_expand(s):
        b = grad_order(s)
        cols = pl.ds(pl.multiple_of(b * BLOCK, BLOCK), BLOCK)
        g_exp[0, cols, :] = dot_tn(z2[:, cols], slope[...]).astype(NARROW)

        due_at("grow", s)

    loop(blocks, grad_expand)

    for j in range(4):
        gat(0, row_own, z2, j).wait_send()

    def middle_back(i):
        r = pl.ds(pl.multiple_of(i * 64, 64), 64)
        grad = red_rows(0, r)
        unit = n2[r, :]
        sums[4 * 8 : 5 * 8, :] += fold(grad * unit)
        sums[5 * 8 : 6 * 8, :] += fold(grad)
        dx1 = c_own[r, :].astype(WIDE) + norm_back(grad, vec[4:5, :], unit, r2[r, :])
        sums[3 * 8 : 4 * 8, :] += fold(dx1 * att[r, :])
        n2[r, :] = dx1
        grad_att = (vec[3:4, :] * dx1).astype(NARROW)
        row_own[r, :] = grad_att
        sums[2 * 8 : 3 * 8, :] += fold(grad_att.astype(WIDE))

    in_halves(0, 1, row_own, da, middle_back)

    def shrink(s):
        r = rows_of(red_block(s))
        m_acc[...] = dot_nt(h[r, :], w_shr[0])
        red_step(1, s)

    dk[...] = jnp.zeros_like(dk)
    dv[...] = jnp.zeros_like(dv)
    lane = lax.broadcasted_iota(jnp.int32, (1, C), 1)

    def grad_mix(s):
        b = grad_order(s)
        cols = pl.ds(pl.multiple_of(b * BLOCK, BLOCK), BLOCK)
        g_mix[0, cols, :] = dot_tn(da[:, cols], o[...]).astype(NARROW)
        grad_block_done(MIX, b)

    def attend_back(s):
        @pl.when(s == 2)
        def _():
            loop(nt, shrink)

        gat_wait(1, row_own, da, s)

        @pl.when(s == 2)
        def _():
            red(1, 2).start()
            red(1, 3).start()

        i = red_block(nt - 1 - s)
        r = rows_of(i)
        w = window(i)
        do = dot(da[r, :], w_mix[0]).astype(NARROW)
        dot_ = do.T.astype(WIDE)
        whole = []
        for hh in range(heads):
            whole.append(jnp.broadcast_to(inv[i, hh : hh + 1, :], (HEAD, BLOCK)))
        scaled = dot_ * jnp.concatenate(whole, 0)
        delta = scaled * ot[i]
        scaled_t = scaled.astype(NARROW)
        natural = scaled_t.T.astype(WIDE)
        queries = q[r, :].astype(WIDE)
        back_q = []

        def grad_scores(hh):
            cols = slice(hh * BLOCK, (hh + 1) * BLOCK)
            here = (lane >= hh * HEAD) & (lane < (hh + 1) * HEAD)
            q_split[cols, :] = jnp.where(here, queries, 0.0).astype(NARROW)
            do_split[cols, :] = jnp.where(here, natural, 0.0).astype(NARROW)
            shift = jnp.sum(delta[hh * HEAD : (hh + 1) * HEAD, :], 0, keepdims=True)
            grads_o = head_rows(scaled_t, hh)
            for c in range(parts):
                place = slice(c * LANES, (c + 1) * LANES)
                grad_p = dot(v[part(i, c), :], grads_o)
                ds[place, cols] = (probs[i, place, cols].astype(WIDE) * (grad_p - shift)).astype(NARROW)

        def grad_queries(hh):
            cols = slice(hh * BLOCK, (hh + 1) * BLOCK)
            back_q.append(dot(kt[hh * HEAD : (hh + 1) * HEAD, w], ds[:, cols]))

        grad_scores(0)
        for hh in range(1, heads):
            grad_scores(hh)
            grad_queries(hh - 1)
        grad_queries(heads - 1)
        grad_q = (jnp.concatenate(back_q, 0) * scaling).astype(NARROW).T
        dqkv[r, 0:half] = grad_q[:, 0:half]
        dqkv[r, width : width + half] = grad_q[:, half:C]
        for c in range(WINDOW // BLOCK):
            place = slice(c * BLOCK, (c + 1) * BLOCK)
            there = pl.ds(pl.multiple_of((i // 2) * BLOCK + c * BLOCK, BLOCK), BLOCK)
            dk[there, :] += dot(ds[place, :], q_split[...])
            dv[there, :] += dot(probs[i, place, :], do_split[...])

        due_at("back", s)

    loop(nt, attend_back)

    def round_kv(i):
        r = pl.ds(pl.multiple_of(i * 128, 128), 128)
        grad_k = dk[r, :].astype(NARROW)
        grad_v = dv[r, :].astype(NARROW)
        for p in range(2):
            here = slice(p * half, (p + 1) * half)
            dqkv[r, p * width + half : p * width + 2 * half] = grad_k[:, here]
            dqkv[r, p * width + 2 * half : (p + 1) * width] = grad_v[:, here]

    loop(T // 128, round_kv)

    def grad_qkv(s):
        b = grad_order(s)
        cols = pl.ds(pl.multiple_of(b * BLOCK, BLOCK), BLOCK)
        both = dot_tn(z1[:, cols], dqkv[...]).astype(NARROW)
        for p in range(2):
            grads[p][0, cols, :] = both[:, p * width : (p + 1) * width]
            grad_block_done(p, b)

    def first_back(s):
        r = rows_of(red_block(s))
        acc[...] = dot_nt(dqkv[r, 0:width], w_ha[0]) + dot_nt(dqkv[r, width : 2 * width], w_hb[0])
        red_step(0, s)

    loop(nt, first_back)
    loop(blocks, grad_mix)
    loop(blocks, grad_qkv)

    def sum_biases(i):
        r = pl.ds(pl.multiple_of(i * 128, 128), 128)
        for p in range(2):
            here = slice(p * half, (p + 1) * half)
            bias_sums[0:8, here] += fold(dqkv[r, p * width : p * width + half].astype(WIDE))
            bias_sums[8:16, here] += fold(dqkv[r, p * width + 2 * half : (p + 1) * width].astype(WIDE))

    loop(T // 128, sum_biases)
    due("heads")

    for j in range(4):
        gat(1, row_own, da, j).wait_send()

    def finish_y(i):
        r = pl.ds(pl.multiple_of(i * 64, 64), 64)
        m = red_rows(1, r) + vec[6:7, :]
        dy = c_own[r, :].astype(WIDE)
        sums[7 * 8 : 8 * 8, :] += fold(dy * m)
        sums[6 * 8 : 7 * 8, :] += fold((vec[7:8, :] * dy).astype(NARROW).astype(WIDE))
        row_own[r, :] = (x1[r, :] + vec[7:8, :] * m).astype(NARROW)

    in_halves(1, 2, row_own, dm, finish_y)

    due("y")
    def finish_dx(i):
        r = pl.ds(pl.multiple_of(i * 64, 64), 64)
        grad = red_rows(0, r)
        unit = n1[r, :]
        sums[0 * 8 : 1 * 8, :] += fold(grad * unit)
        sums[1 * 8 : 2 * 8, :] += fold(grad)
        dx = n2[r, :] + norm_back(grad, vec[0:1, :], unit, r1[r, :])
        x_own[r, :] = dx.astype(NARROW)

    in_halves(0, 3, x_own, z2, finish_dx)
    due("dx")

    for j in range(8):
        vec_parts[t, j : j + 1, :] = jnp.sum(sums[j * 8 : (j + 1) * 8, :], 0, keepdims=True)

    def vec_to(kk):
        return to_tensor(vec_parts.at[t], vec_parts.at[t], vs_s.at[kk], vs_r.at[kk], (t + kk) % nt)

    loop(nt - 1, lambda i: vec_to(i + 1).start())
    gat_forward(2, row_own, dm)
    loop(nt - 1, lambda i: vec_to(i + 1).wait_recv())
    total = vec_parts[0]
    for j in range(1, nt):
        total = total + vec_parts[j]
    lines = [jnp.sum(bias_sums[j * 8 : (j + 1) * 8, :], 0, keepdims=True) for j in range(3)]
    lines = jnp.concatenate(lines + [jnp.zeros((5, F), WIDE)], 0)
    high = lines.astype(NARROW).astype(WIDE)
    lines = jnp.concatenate([high, lines - high], 0)

    def pack(i):
        both = dot_nt(jnp.where(of_peer(i), lines, 0.0).astype(NARROW), comb[...])
        small_send[i, 8:16, :] = both[0:8, :] + both[8:16, :]

    loop(nd, pack)
    if cs == LANES:
        for i in range(nd):
            small_send[i, 0:8, :] = total[:, i * cs : (i + 1) * cs]
    else:
        vec_high = total.astype(NARROW)
        vec_low = (total - vec_high.astype(WIDE)).astype(NARROW)

        def pack_vec(i):
            row = lax.broadcasted_iota(jnp.int32, (D, LANES), 0)
            low = lax.broadcasted_iota(jnp.int32, (D, LANES), 1)
            pick = jnp.where((row == i * cs + low) & (low < cs), 1.0, 0.0).astype(NARROW)
            small_send[i, 0:8, :] = dot(vec_high, pick) + dot(vec_low, pick)

        loop(nd, pack_vec)

    def grad_small(kk):
        peer = (me + kk) % nd
        return to_dp(small_send.at[peer], small_recv.at[me], gs_s.at[kk], gs_r.at[kk], peer)

    loop(nd - 1, lambda i: grad_small(i + 1).start())
    small_recv[me] = small_send[me]
    due("pack")
    gat_forward(3, x_own, z2)
    due("last")
    loop(nd - 1, lambda i: grad_small(i + 1).wait_recv())
    out_small[...] = lax.fori_loop(
        1, nd, lambda i, s: s + small_recv[i], small_recv[0]
    )

    def ag_drain(a, d):
        for late in (False, True) if turned[a] else (False,):

            @pl.when((mz + 1 < no) & (mz + 1 >= d))
            def _():
                ag_right(a, d, late).wait_send()

            @pl.when((mz > 0) & (mz + d <= no))
            def _():
                ag_left(a, d, late).wait_send()

    keep = []
    for g, src, ref, out in ((2, row_own, dm, out_y), (3, x_own, z2, out_dx)):
        gat(g, src, ref, 0).wait_recv()
        gat(g, src, ref, 1).wait_recv()
        keep.append(load(8 + g, ref, out))
        keep[-1].start()
        for j in range(4):
            gat(g, src, ref, j).wait_send()
    for a in range(5):
        peers(functools.partial(ag_drain, a))
        ag_own(a).wait_send()
        peers(lambda i: ag_x(a, (mz + i) % no).wait_send())
        loop(no - 1, lambda i: rs_z(a, i + 1).wait_send())
        loop(no, lambda i: rs_x(a, i).wait_send())
    loop(nd - 1, lambda i: small(i + 1).wait_send())
    loop(nd - 1, lambda i: grad_small(i + 1).wait_send())
    loop(nt - 1, lambda i: vec_to(i + 1).wait_send())
    for copy in keep:
        copy.wait()


def layer(nd, nt, tokens, segments, cotangent, heads, mixer, expand, shrink, vector, biases, offset):
    T, D = tokens.shape
    C, F = heads.shape[2], expand.shape[1]
    cs, no, own = D // nd, nd // 2, T // nt
    sds = jax.ShapeDtypeStruct
    dma = pltpu.SemaphoreType.DMA

    def nar(*shape):
        return pltpu.VMEM(shape, NARROW)

    def wid(*shape):
        return pltpu.VMEM(shape, WIDE)

    shapes = ((1, 3 * C // 2), (1, 3 * C // 2), (1, C), (1, F), (1, F))
    scratch = [wid(*x.shape) for x in (mixer, shrink)]
    scratch += [nar(m, D, w) for m, w in shapes]
    scratch += [nar(T, D), nar(T, D), nar(own, D), nar(own, D), wid(T, LANES)]
    scratch += [wid(SMALL_ROWS, D), wid(SMALL_ROWS, F), wid(own, D), wid(own, 1)]
    scratch += [nar(T, C), nar(T, C), nar(T, C), nar(C, T), nar(C, T)]
    scratch += [nar(nt, WINDOW, (C // HEAD) * BLOCK)]
    scratch += [wid(nt, 8, BLOCK), wid(nt, C, BLOCK), nar(T, C), wid(own, D)]
    scratch += [wid(own, D), wid(own, D), wid(own, D), wid(own, 1)]
    scratch += [nar(T, D), nar(T, F), nar(T, F), nar(T, D)]
    scratch += [nar(WINDOW, (C // HEAD) * BLOCK), nar((C // HEAD) * BLOCK, C), nar((C // HEAD) * BLOCK, C)]
    scratch += [nar(T, 3 * C), wid(T, C), wid(T, C), nar(LANES, F)]
    scratch += [wid(64, D), wid(24, F), nar(own, D)]
    scratch += [nar(2, own, D), nar(2, own, D), nar(own, D), nar(own, D)]
    scratch += [wid(own, D), nar(2, own, D), nar(2, own, D), nar(own, D), nar(own, D)]
    scratch += [nar(m, D, w) for m, w in shapes]
    scratch += [nar(no, m, cs, w) for m, w in shapes]
    scratch += [nar(no - 1, m, cs, w) for m, w in shapes]
    scratch += [wid(nd, SMALL_ROWS, LANES), wid(nt, 8, D), wid(nd, SMALL_ROWS, LANES), wid(nd, SMALL_ROWS, LANES)]
    scratch += [dma((12,))]
    scratch += [dma((5, no + 1)) for _ in range(8)] + [dma((5, no)) for _ in range(6)]
    scratch += [dma((nd,)) for _ in range(4)]
    scratch += [dma((nt,)) for _ in range(2)]
    scratch += [dma((2, 4)), dma((2, 4)), dma((4, 4)), dma((4, 4))]

    anywhere = pl.BlockSpec(memory_space=pl.ANY)
    vmem = pl.BlockSpec(memory_space=pltpu.VMEM)
    return pl.pallas_call(
        functools.partial(kernel, nd, nt),
        out_shape=[
            sds((T, D), NARROW),
            sds((T, D), NARROW),
            *[sds((m, cs, w), WIDE) for m, w in shapes],
            sds((SMALL_ROWS, LANES), WIDE),
        ],
        in_specs=[anywhere, vmem] + [anywhere] * 5 + [vmem] * 3,
        out_specs=[anywhere, anywhere] + [vmem] * 6,
        scratch_shapes=scratch,
        compiler_params=pltpu.CompilerParams(
            collective_id=0, has_side_effects=True, vmem_limit_bytes=VMEM_LIMIT
        ),
    )(tokens, segments.reshape(1, T), cotangent, heads, mixer, expand, shrink, vector, biases, offset)


def update_kernel(*refs):
    raw_y, raw_dx = refs[:2]
    sources, refs = refs[2:29], refs[29:]
    out_y, out_dx = refs[:2]
    targets, refs = refs[2:16], refs[16:]
    held, news, t_mix, t_shr = refs[:27], refs[27:41], refs[41], refs[42]
    held_y, held_dx, sem = refs[43:]
    first = (0, 1, 6, 13, 20, 3, 9, 16, 23)
    loads = [pltpu.make_async_copy(sources[i], held[i], sem.at[i]) for i in range(27)]
    take = [
        pltpu.make_async_copy(raw_y, held_y, sem.at[27]),
        pltpu.make_async_copy(raw_dx, held_dx, sem.at[28]),
    ]
    for i in first:
        loads[i].start()
    for i in (4, 11, 18, 25, 2, 8, 15, 22):
        loads[i].start()
    for copy in take:
        copy.start()
    for i in (5, 7, 10, 12, 14, 17, 19, 21, 24, 26):
        loads[i].start()
    keep = [
        pltpu.make_async_copy(held_y, out_y, sem.at[43]),
        pltpu.make_async_copy(held_dx, out_dx, sem.at[44]),
    ]
    grads, state = held[:6], held[6:]
    stores = [pltpu.make_async_copy(news[i], targets[i], sem.at[29 + i]) for i in range(14)]

    def arrive(slot, source=None):
        if source is not None:
            loads[source].wait()
        for j in range(3):
            loads[6 + slot + 7 * j].wait()

    def update(slot, gradient, decay_rate, at=lambda ref: ref):
        master, moment, square = (at(state[slot + 7 * j])[...] for j in range(3))
        moment = BETA_ONE * moment + (1.0 - BETA_ONE) * gradient
        square = BETA_TWO * square + (1.0 - BETA_TWO) * gradient * gradient
        at(news[slot + 7])[...] = moment
        change = moment * (1 / CORRECT_ONE) / (jnp.sqrt(square * (1 / CORRECT_TWO)) + ADAM_EPS)
        at(news[slot])[...] = change + decay_rate * master

    def by_rows(slot, gradient, step):
        def one(c):
            r = pl.ds(pl.multiple_of(c * step, step), step)
            update(slot, gradient[r, :], WEIGHT_DECAY, lambda ref: ref.at[r, :])

        loop(gradient.shape[0] // step, one)

    def leave(slot):
        stores[slot].start()
        stores[slot + 7].start()

    loads[1].wait()
    arrive(0, 0)
    half = grads[0].shape[2] // 3
    for j in range(3):
        here = slice(j * half, (j + 1) * half)
        whole = jnp.concatenate([grads[0][0, :, here], grads[1][0, :, here]], 1)
        update(0, whole, WEIGHT_DECAY, lambda ref: ref.at[j])
    leave(0)
    arrive(3, 3)
    by_rows(3, grads[3].at[0], min(32, grads[3].shape[1]))
    leave(3)
    for j in range(2):
        take[j].wait()
        keep[j].start()
    arrive(5, 4)
    t_shr[...] = grads[4][0].T
    by_rows(5, t_shr, 256)
    leave(5)
    arrive(2, 2)
    t_mix[...] = grads[2][0].T
    by_rows(2, t_mix, 256)
    leave(2)
    loads[5].wait()
    small = grads[5]
    for slot, rows in ((1, slice(8, 10)), (4, slice(10, 11)), (6, slice(0, 8))):
        arrive(slot)
        update(slot, small[rows, 0 : state[slot].shape[1]], 0.0)
        leave(slot)
    for copy in keep + stores:
        copy.wait()


def shards(nd, nt, tokens, segments, cotangent, *state):
    heads, biases, mixer, expand, offset, shrink, vector = state[:7]
    flat = list(state)
    for j in range(0, 21, 7):
        flat[j + 1] = state[j + 1].reshape(2, -1)
        flat[j + 4] = state[j + 4].reshape(1, -1)
    results = layer(nd, nt, tokens, segments, cotangent, heads, mixer, expand, shrink, vector, flat[1], flat[4])
    anywhere = pl.BlockSpec(memory_space=pl.ANY)
    sds = jax.ShapeDtypeStruct
    outs = pl.pallas_call(
        update_kernel,
        out_shape=[sds(x.shape, x.dtype) for x in results[:2]] + [sds(x.shape, WIDE) for x in flat[:7]] * 2,
        in_specs=[anywhere] * 29,
        out_specs=[anywhere] * 16,
        scratch_shapes=[
            *[pltpu.VMEM(x.shape, WIDE) for x in (*results[2:], *flat, *flat[:7], *flat[:7], mixer, shrink)],
            pltpu.VMEM(results[0].shape, NARROW),
            pltpu.VMEM(results[1].shape, NARROW),
            pltpu.SemaphoreType.DMA((45,)),
        ],
        compiler_params=pltpu.CompilerParams(vmem_limit_bytes=VMEM_LIMIT),
    )(*results, *flat)
    outs = list(outs)
    for j in (2, 9):
        outs[j + 1] = outs[j + 1].reshape(biases.shape)
        outs[j + 4] = outs[j + 4].reshape(offset.shape)
    return tuple(outs)


def solution(mesh):
    matrices = (
        P(None, "dp", "tensor"),
        P(None, "tensor", "dp"),
        P("tensor", "dp"),
        P("dp", "tensor"),
        P("tensor", "dp"),
        P("tensor", "dp"),
        P(None, "dp"),
    )
    rows = P("dp", None)
    return jax.shard_map(
        functools.partial(shards, mesh.shape["dp"], mesh.shape["tensor"]),
        mesh=mesh,
        in_specs=(rows, P("dp"), rows) + matrices * 3,
        out_specs=(rows, rows) + matrices * 2,
        check_vma=False,
    )
```
